32 devices in a mesh: rep: 4 (over y, x), shard: 8 (over z, core).
Axes of the slice: x: 2, y: 2, z: 4, core: 2. Of those that a mesh axis runs over, the one named last changes fastest.
Arguments:
- hidden: bfloat16 [8192, 768], P(('rep', 'shard')), may hold values from -6 to 6
- encoded: bfloat16 [3072, 768], P(('rep', 'shard')), may hold values from -6 to 6
- tok_seg: int32 [4, 2048], P('rep'), may hold values from 0 to 12, as said below
- seg_parent: int32 [4, 13], P('rep'), may hold values from -1 to 4, as said below
- self_qkv: bfloat16 [3, 768, 768], P(None, 'shard'), may hold values from -0.21875 to 0.21875
- self_out: bfloat16 [768, 768], P('shard'), may hold values from -1.5 to 1.5
- cross_qkv: bfloat16 [3, 768, 768], P(None, 'shard'), may hold values from -0.21875 to 0.21875
- cross_out: bfloat16 [768, 768], P('shard'), may hold values from -1.5 to 1.5
- fc_in: bfloat16 [768, 3072], P('shard'), may hold values from -0.21875 to 0.21875
- fc_out: bfloat16 [3072, 768], P('shard'), may hold values from -0.109375 to 0.109375
- proj_bias: bfloat16 [4, 768], P(None, 'shard'), may hold values from -1.5 to 1.5
- out_bias: bfloat16 [3, 768], P(None, 'shard'), may hold values from -1.5 to 1.5
- fc_in_bias: bfloat16 [3072], P('shard'), may hold values from -1.5 to 1.5
- norm_gain: bfloat16 [3, 768], P(None, 'shard'), may hold values from 0.25 to 1.75
- norm_bias: bfloat16 [3, 768], P(None, 'shard'), may hold values from -1.5 to 1.5
- cotangent: bfloat16 [8192, 768], P(('rep', 'shard')), may hold values from -6 to 6
Outputs:
- output: float32 [8192, 768], P(('rep', 'shard'))
- d_hidden: float32 [8192, 768], P(('rep', 'shard'))
- d_encoded: float32 [3072, 768], P(('rep', 'shard'))
- g_self_qkv: float32 [3, 768, 768], P(None, 'shard')
- g_self_out: float32 [768, 768], P('shard')
- g_cross_qkv: float32 [3, 768, 768], P(None, 'shard')
- g_cross_out: float32 [768, 768], P('shard')
- g_fc_in: float32 [768, 3072], P('shard')
- g_fc_out: float32 [3072, 768], P('shard')
- g_proj_bias: float32 [4, 768], P(None, 'shard')
- g_out_bias: float32 [3, 768], P(None, 'shard')
- g_fc_in_bias: float32 [3072], P('shard')
- g_norm_gain: float32 [3, 768], P(None, 'shard')
- g_norm_bias: float32 [3, 768], P(None, 'shard')
The draws below stay inside these ranges and needn't reach their ends.
Inputs may be any that keep to these rules, and one draw needn't show every extreme that they name: `tok_seg`: per tree: segment ids never fall; segment 0 is the first 1024 tokens, segments 1 to 4 branches, 5 to 12 leaves, each at least one token. `seg_parent`: per tree: -1 for segment 0, 0 for segments 1 to 4, and each of segments 1 to 4 is the parent of two of the segments 5 to 12.
All inputs are finite; a program needn't handle non-finite values.
Results may differ from the reference program's by a relative error of at most 0.04.
Values may be sent and summed in bfloat16 or wider, within the bound.
A program may use at most 256 MiB of HBM per device.

```python
import math
import jax
import jax.numpy as jnp
from jax import lax

D = 768
HEADS = 12
HDIM = 64
FF = 3072
SEGS = 13
TREES = 4
TREE = 2048
TOKENS = 8192
FRAMES = 768
ENC_ROWS = 3072


def tree_layout(key):

    def one_tree(tree_key):
        key_branch, key_leaf, key_order = jax.random.split(tree_key, 3)
        branch_shift = jax.random.randint(key_branch, (2,), -(TREE // 32), TREE // 32 + 1)
        branch_lengths = TREE // 16 + jnp.stack([branch_shift[0], -branch_shift[0], branch_shift[1], -branch_shift[1]])
        leaf_shift = jax.random.randint(key_leaf, (4,), -(TREE // 64), TREE // 64 + 1)
        leaf_lengths = TREE // 32 + jnp.stack([leaf_shift, -leaf_shift], axis=1).reshape(8)
        lengths = jnp.concatenate([jnp.full((1,), TREE // 2, dtype=jnp.int32), branch_lengths.astype(jnp.int32), leaf_lengths.astype(jnp.int32)])
        order = jax.random.permutation(key_order, 8).astype(jnp.int32)
        parents = jnp.concatenate([jnp.array([-1, 0, 0, 0, 0], dtype=jnp.int32), 1 + order // 2])
        ends = jnp.cumsum(lengths)
        positions = jnp.arange(TREE, dtype=jnp.int32)
        segments = jnp.sum((positions[:, None] >= ends[None, :]).astype(jnp.int32), axis=1)
        return (segments.astype(jnp.int32), parents.astype(jnp.int32))
    tree_keys = jax.random.split(jax.random.fold_in(key, 101), TREES)
    return jax.vmap(one_tree)(tree_keys)


def draw_tok_seg(key, part):
    return tree_layout(key)[0]


def draw_seg_parent(key, part):
    return tree_layout(key)[1]


def shard_levels(stream_key, shape, shards, low, top_value):
    level = 1.0
    for position, shards_of in shards:
        draws = jax.random.uniform(jax.random.fold_in(jax.random.fold_in(stream_key, 6), position), (shards_of,), jnp.float32, low / len(shards), top_value / len(shards))
        level = level * jnp.repeat(jnp.exp(draws), shape[position] // shards_of).reshape((-1,) + (1,) * (len(shape) - 1 - position))
    return level


def gaussian(stream_key, extent, spread, most, pieces=(), held_as=jnp.bfloat16):
    factor_of = shard_levels(stream_key, extent, pieces, -0.22, 0.18) if pieces else 1.0
    values = jax.random.normal(stream_key, extent, jnp.float32) * spread * factor_of
    return jnp.minimum(jnp.maximum(values, -most), most).astype(held_as)


def setup_inputs(seed: int = 0) -> dict:
    seeds = jax.random.split(jax.random.key(seed), 17)
    hidden = gaussian(seeds[0], (TOKENS, D), 1.0, 6.0, ((0, 32),))
    encoded = gaussian(seeds[1], (ENC_ROWS, D), 1.0, 6.0, ((0, 32),))
    tok_seg = draw_tok_seg(jax.random.fold_in(seeds[16], 71), 0)
    seg_parent = draw_seg_parent(jax.random.fold_in(seeds[16], 71), 0)
    self_qkv = gaussian(seeds[4], (3, D, D), D ** -0.5, 0.21875, ((1, 8),))
    self_out = gaussian(seeds[5], (D, D), 16 ** -0.5, 1.5, ((0, 8),))
    cross_qkv = gaussian(seeds[6], (3, D, D), D ** -0.5, 0.21875, ((1, 8),))
    cross_out = gaussian(seeds[7], (D, D), 16 ** -0.5, 1.5, ((0, 8),))
    fc_in = gaussian(seeds[8], (D, FF), D ** -0.5, 0.21875, ((0, 8),))
    fc_out = gaussian(seeds[9], (FF, D), FF ** -0.5, 0.109375, ((0, 8),))
    proj_bias = gaussian(seeds[10], (4, D), 0.3, 1.5, ((1, 8),))
    out_bias = gaussian(seeds[11], (3, D), 0.3, 1.5, ((1, 8),))
    fc_in_bias = gaussian(seeds[12], (FF,), 0.3, 1.5, ((0, 8),))
    norm_gain = jnp.clip(1.0 + 0.15 * jax.random.normal(seeds[13], (3, D), jnp.float32), 0.25, 1.75).astype(jnp.bfloat16)
    norm_bias = gaussian(seeds[14], (3, D), 0.3, 1.5, ((1, 8),))
    cotangent = gaussian(seeds[15], (TOKENS, D), 1.0, 6.0, ((0, 32),))
    return {"hidden": hidden, "encoded": encoded, "tok_seg": tok_seg, "seg_parent": seg_parent, "self_qkv": self_qkv, "self_out": self_out, "cross_qkv": cross_qkv, "cross_out": cross_out, "fc_in": fc_in, "fc_out": fc_out, "proj_bias": proj_bias, "out_bias": out_bias, "fc_in_bias": fc_in_bias, "norm_gain": norm_gain, "norm_bias": norm_bias, "cotangent": cotangent}


EPS = 1e-05
NEGATIVE = -1e+30
HIGH = lax.Precision.HIGHEST

@jax.custom_vjp
def low(v):
    return lax.optimization_barrier(v.astype(jnp.bfloat16)).astype(jnp.float32)

@jax.custom_vjp
def low_back(v):
    return v

def low_keep(v):
    return (low(v), None)

def low_pass(kept, grad):
    return (grad,)

def back_keep(v):
    return (v, None)

def back_low(kept, grad):
    return (low(grad),)
low.defvjp(low_keep, low_pass)
low_back.defvjp(back_keep, back_low)

def both_ways(value):
    return low(low_back(value))

def layer_norm(values, gain, shift):
    centered = values - lax.optimization_barrier(jnp.mean(values, axis=-1, keepdims=True))
    variance = lax.optimization_barrier(jnp.mean(centered * centered, axis=-1, keepdims=True))
    return centered * lax.rsqrt(variance + EPS) * gain + shift

def matmul(left, right):
    return jnp.matmul(left, right, precision=HIGH)

def ancestry(parents):
    segment_ids = jnp.arange(SEGS, dtype=jnp.int32)
    grandparent = jnp.where(parents >= 0, parents[jnp.maximum(parents, 0)], -1)
    same = segment_ids[None, :] == segment_ids[:, None]
    parent_of = segment_ids[None, :] == parents[:, None]
    grand_of = segment_ids[None, :] == grandparent[:, None]
    return same | parent_of | grand_of

def self_attention(queries, keys, values, segments, parents):
    score_scale = HDIM ** (-0.5)
    block_rows = math.gcd(TREE, 512)

    def one_tree(inputs):
        tree_q, tree_k, tree_v, tree_seg, tree_par = inputs
        reach = ancestry(tree_par)
        positions = jnp.arange(TREE, dtype=jnp.int32)
        key_heads = tree_k.reshape(TREE, HEADS, HDIM)
        value_heads = tree_v.reshape(TREE, HEADS, HDIM)

        def per_block(block_inputs):
            block_q, block_pos, block_seg = block_inputs
            scores = low_back(jnp.einsum('qhd,khd->hqk', block_q, key_heads, precision=HIGH) * score_scale)
            visible = reach[block_seg][:, tree_seg] & (positions[None, :] <= block_pos[:, None])
            scores = jnp.where(visible[None], scores, NEGATIVE)
            weights = low(jax.nn.softmax(scores, axis=-1))
            return jnp.einsum('hqk,khd->qhd', weights, value_heads, precision=HIGH).reshape(block_rows, D)
        count = TREE // block_rows
        out_blocks = lax.map(jax.checkpoint(per_block), (tree_q.reshape(count, block_rows, HEADS, HDIM), positions.reshape(count, block_rows), tree_seg.reshape(count, block_rows)))
        return out_blocks.reshape(TREE, D)
    return lax.map(one_tree, (queries, keys, values, segments, parents))

def cross_attention(queries, keys, values):
    score_scale = HDIM ** (-0.5)
    block_rows = math.gcd(TREE, 512)

    def one_tree(inputs):
        tree_q, tree_k, tree_v = inputs
        key_heads = tree_k.reshape(FRAMES, HEADS, HDIM)
        value_heads = tree_v.reshape(FRAMES, HEADS, HDIM)

        def per_block(block_q):
            scores = low_back(jnp.einsum('qhd,khd->hqk', block_q, key_heads, precision=HIGH) * score_scale)
            weights = low(jax.nn.softmax(scores, axis=-1))
            return jnp.einsum('hqk,khd->qhd', weights, value_heads, precision=HIGH).reshape(block_rows, D)
        count = TREE // block_rows
        out_blocks = lax.map(jax.checkpoint(per_block), tree_q.reshape(count, block_rows, HEADS, HDIM))
        return out_blocks.reshape(TREE, D)
    return lax.map(one_tree, (queries, keys, values))

def reference(hidden, encoded, tok_seg, seg_parent, self_qkv, self_out, cross_qkv, cross_out, fc_in, fc_out, proj_bias, out_bias, fc_in_bias, norm_gain, norm_bias, cotangent):
    hidden_f = hidden.astype(jnp.float32).reshape(TREES, TREE, D)
    encoded_f = encoded.astype(jnp.float32).reshape(TREES, FRAMES, D)
    cot_f = cotangent.astype(jnp.float32).reshape(TREES, TREE, D)
    params = tuple((p.astype(jnp.float32) for p in (self_qkv, self_out, cross_qkv, cross_out, fc_in, fc_out, proj_bias, out_bias, fc_in_bias, norm_gain, norm_bias)))

    def forward(stream, states, weights):
        w_self, w_self_out, w_cross, w_cross_out, w_fc_in, w_fc_out, b_proj, b_out, b_fc_in, gains, shifts = weights
        normed = low(layer_norm(stream, gains[0], shifts[0]))
        queries = both_ways(matmul(normed, w_self[0]) + b_proj[0])
        keys_self = both_ways(matmul(normed, w_self[1]))
        values_self = both_ways(matmul(normed, w_self[2]) + b_proj[1])
        attended = both_ways(self_attention(queries, keys_self, values_self, tok_seg, seg_parent))
        after_self = stream + low_back(matmul(attended, w_self_out) + b_out[0])
        normed_cross = low(layer_norm(after_self, gains[1], shifts[1]))
        cross_queries = both_ways(matmul(normed_cross, w_cross[0]) + b_proj[2])
        cross_keys = both_ways(matmul(states, w_cross[1]))
        cross_values = both_ways(matmul(states, w_cross[2]) + b_proj[3])
        attended_cross = both_ways(cross_attention(cross_queries, cross_keys, cross_values))
        after_cross = after_self + low_back(matmul(attended_cross, w_cross_out) + b_out[1])
        normed_mlp = low(layer_norm(after_cross, gains[2], shifts[2]))
        pre_act = low_back(matmul(normed_mlp, w_fc_in) + b_fc_in)
        activated = low(jax.nn.gelu(pre_act, approximate=False))
        return after_cross + matmul(activated, w_fc_out) + b_out[2]
    result, pullback = jax.vjp(forward, hidden_f, encoded_f, params)
    d_stream, d_states, d_params = pullback(cot_f)
    return (result.reshape(TOKENS, D), d_stream.reshape(TOKENS, D), d_states.reshape(ENC_ROWS, D), d_params[0], d_params[1], d_params[2], d_params[3], d_params[4], d_params[5], d_params[6], d_params[7], d_params[8], d_params[9], d_params[10])
```

```python
import functools
import math

import jax
import jax.numpy as jnp
from jax import lax
from jax.experimental import pallas as pl
from jax.experimental.pallas import tpu as pltpu
from jax.sharding import PartitionSpec as P

HEADS = 12
EPS = 1e-05
NEGATIVE = -1e30
MESH = pl.DeviceIdType.MESH
UNITS = 4
SMALL_ROWS = 32
GRAD_ROWS = 24
BF = jnp.bfloat16
F32 = jnp.float32


def flip_bit(index, bit):
    size = 1 << bit
    return index + size * (1 - 2 * ((index // size) % 2))


def pick(core, first, second):
    return first + core * (second - first)


class Place:
    def __init__(self, shards, reps):
        self.shards, self.reps = shards, reps
        self.rep = lax.axis_index("rep")
        self.shard = lax.axis_index("shard")
        self.pos = self.shard // 2
        self.core = self.shard % 2
        self.line = shards // 2
        self.bits = reps.bit_length() - 1

    def partner(self):
        return (self.rep, self.shard + 1 - 2 * self.core)

    def along(self, pos):
        return (self.rep, pos * 2 + self.core)

    def flipped(self, index, step):
        return pick(
            self.core, flip_bit(index, step), flip_bit(index, self.bits - 1 - step)
        )

    def subset(self, index, steps):
        for step in steps:
            index = self.flipped(index, step)
        return index


def subsets(steps):
    found = [()]
    for step in steps:
        found = found + [more + (step,) for more in found]
    return found


def remote(src, dst, send, recv, device):
    return pltpu.make_async_remote_copy(
        src_ref=src, dst_ref=dst, send_sem=send, recv_sem=recv,
        device_id=device, device_id_type=MESH,
    )


def greet(devices, conditions):
    barrier = pltpu.get_barrier_semaphore()
    count = 0
    for device, condition in zip(devices, conditions):
        if condition is None:
            pl.semaphore_signal(barrier, inc=1, device_id=device, device_id_type=MESH)
            count = count + 1
        else:
            @pl.when(condition)
            def _(device=device):
                pl.semaphore_signal(barrier, inc=1, device_id=device, device_id_type=MESH)
            count = count + jnp.where(condition, 1, 0)
    pl.semaphore_wait(barrier, count)


def cond(condition, action):
    @pl.when(condition)
    def _():
        action()


def nn(a, b):
    return lax.dot_general(a, b, (((1,), (0,)), ((), ())), preferred_element_type=F32)


def nt(a, b):
    return lax.dot_general(a, b, (((1,), (1,)), ((), ())), preferred_element_type=F32)


def normalise(values):
    centered = values - jnp.mean(values, axis=-1, keepdims=True)
    scale = lax.rsqrt(jnp.mean(centered * centered, axis=-1, keepdims=True) + EPS)
    return centered * scale, scale


def norm_back(hat, scale, gain, grad):
    scaled = grad * gain
    mean = jnp.mean(scaled, axis=-1, keepdims=True)
    along = jnp.mean(scaled * hat, axis=-1, keepdims=True)
    return (scaled - mean - hat * along) * scale


def column_sums(values):
    return jnp.sum(values, axis=0, keepdims=True)


def pair_rows(values, pair):
    both = values[:, pair * 128 : pair * 128 + 128]
    first = lax.broadcasted_iota(jnp.int32, both.shape, 1) < 64
    zero = jnp.zeros_like(both)
    return jnp.concatenate([jnp.where(first, both, zero), jnp.where(first, zero, both)], axis=0)


def unpair(turned):
    both = jnp.transpose(turned)
    rows = both.shape[0] // 2
    first = lax.broadcasted_iota(jnp.int32, (rows, 128), 1) < 64
    return jnp.where(first, both[:rows], both[rows:])


def earlier(block, rows):
    key = lax.broadcasted_iota(jnp.int32, (block, 2 * rows), 0)
    query = lax.broadcasted_iota(jnp.int32, (block, 2 * rows), 1)
    return key <= jnp.where(query >= rows, query - rows, query)


def attend_start(top, total, acc):
    top[...] = jnp.full(top.shape, NEGATIVE, F32)
    total[...] = jnp.zeros(total.shape, F32)
    acc[...] = jnp.zeros(acc.shape, F32)


def attend_block(queries, keys, turned_values, hot, top, total, acc, diagonal):
    for pair in range(queries.shape[0]):
        lanes = slice(pair * 128, pair * 128 + 128)
        left = keys[:, lanes]
        if hot is not None:
            left = jnp.concatenate([left, hot], axis=1)
        scores = nt(left, queries[pair])
        if diagonal:
            scores = jnp.where(earlier(left.shape[0], scores.shape[1] // 2), scores, NEGATIVE)
        before = top[pair : pair + 1, :]
        after = jnp.maximum(before, jnp.max(scores, axis=0, keepdims=True))
        factor = jnp.exp(before - after)
        weights = jnp.exp(scores - after)
        top[pair : pair + 1, :] = after
        total[pair : pair + 1, :] = total[pair : pair + 1, :] * factor + jnp.sum(weights, axis=0, keepdims=True)
        acc[pair] = acc[pair] * factor + nn(turned_values[lanes, :], weights.astype(BF))


def attend_finish(top, total, acc, lse, out):
    for pair in range(acc.shape[0]):
        sums = total[pair : pair + 1, :]
        lse[pair : pair + 1, :] = top[pair : pair + 1, :] + jnp.log(sums)
        out[:, pair * 128 : pair * 128 + 128] = unpair(acc[pair] / sums)


def attend_back_block(queries, grads, keys, values, turned_keys, hot, lse, delta, grad_q, grad_k, grad_v, diagonal):
    for pair in range(queries.shape[0]):
        lanes = slice(pair * 128, pair * 128 + 128)
        left = keys[:, lanes]
        if hot is not None:
            left = jnp.concatenate([left, hot], axis=1)
        scores = nt(left, queries[pair])
        if diagonal:
            scores = jnp.where(earlier(left.shape[0], scores.shape[1] // 2), scores, NEGATIVE)
        probs = jnp.exp(scores - lse[pair : pair + 1, :])
        grad_probs = nt(values[:, lanes], grads[pair])
        grad_scores = (probs * (grad_probs - delta[pair : pair + 1, :])).astype(BF)
        grad_v[:, lanes] = nn(probs.astype(BF), grads[pair]).astype(BF)
        grad_k[:, lanes] = nn(grad_scores, queries[pair, :, 0:128]).astype(BF)
        grad_q[pair] += nn(turned_keys[lanes, :], grad_scores)


def deltas(grad, out, delta, pairs):
    turned = jnp.transpose(grad.astype(F32) * out)
    for pair in range(pairs):
        at = pair * 128
        one = jnp.sum(turned[at : at + 64], axis=0, keepdims=True)
        two = jnp.sum(turned[at + 64 : at + 128], axis=0, keepdims=True)
        delta[pair : pair + 1, :] = jnp.concatenate([one, two], axis=1)


def store_owners(grads, group, unit, matrix, shards):
    rows = matrix.shape[0] // shards
    for s in range(shards):
        grads[group, s // 2, s % 2, unit * rows : (unit + 1) * rows, :] = matrix[s * rows : (s + 1) * rows].astype(BF)


def erf_parts(pre):
    cdf = 0.5 * (1.0 + lax.erf(pre * (0.5**0.5)))
    slope = cdf + pre * jnp.exp(-0.5 * pre * pre) * (1.0 / math.sqrt(2.0 * math.pi))
    return cdf, slope


G_OUT, G_IN, G_CROSS, G_SELF = range(4)
V_PROJ, V_OUT, V_GAIN, V_SHIFT, V_IN = 0, 4, 7, 10, 13


def shape_of(kind, *shape):
    return jax.ShapeDtypeStruct(shape, kind)


SELF, CROSS, FC_IN, FC_OUT, HIDDEN, ENCODED, SMALL = range(7)
WEIGHTS = (SELF, CROSS, FC_IN, FC_OUT)


def forward_kernel(
    shards, reps, *refs,
):
    ins, (segs, parents, cotangent) = refs[:7], refs[7:10]
    (result, grad_across, grads, keys, values, queries, hot, lse, att, c_queries, c_keys, c_values, c_lse, catt,
     after_self, normed1, sums, params, keep_self, keep_cross, keep_hidden, keep_states) = refs[10:32]
    (w_self, w_cross, w_in, w_out, hidden, states, small_all, bias_in,
     kbuf, vbuf, turned, c_turned, top, total, acc, grad_n2, held, gbuf_in, gbuf_out,
     k_sem, v_sem, g_sem, keep_sem, own_sem, mate_send, mate_recv, line_send, line_recv, rep_send, rep_recv,
     far_send, far_recv, small_send, small_recv) = refs[32:]
    outs = (w_self, w_cross, w_in, w_out, hidden, states, small_all)
    here = Place(shards, reps)
    line, bits = here.line, here.bits
    pos, core, rep, shard = here.pos, here.core, here.rep, here.shard
    rows, width = cotangent.shape
    frames = states.shape[0]
    strip = width * UNITS // reps
    w_rows = ins[SELF].shape[1]


    def block(refs_, item, s):
        ref = refs_[item]
        if item in (SELF, CROSS):
            return ref.at[:, pl.ds(pl.multiple_of(s * w_rows, 16), w_rows), :]
        n = ins[item].shape[0]
        return ref.at[pl.ds(pl.multiple_of(s * n, 16), n), :]

    def piece(refs_, item, r, s):
        if item == ENCODED:
            return block(refs_, item, s)
        ref = refs_[item]
        unit = r % UNITS
        at = 0 if reps == UNITS else pl.multiple_of((r // UNITS) * strip, 128)
        columns = pl.ds(at, strip)
        if item in (SELF, CROSS):
            return ref.at[unit, pl.ds(pl.multiple_of(s * w_rows, 16), w_rows), columns]
        if item == FC_IN:
            return ref.at[
                pl.ds(pl.multiple_of(s * w_rows, 16), w_rows), pl.ds(pl.multiple_of(unit * width + at, 128), strip)
            ]
        return ref.at[pl.ds(pl.multiple_of(s * UNITS * w_rows + unit * w_rows, 16), w_rows), columns]

    mate = here.partner()
    greet(
        [(rep, (shard + d) % shards) for d in range(1, shards)]
        + [(flip_bit(rep, bit), shard) for bit in range(bits)],
        [None] * (shards - 1 + bits),
    )

    own = [pltpu.make_async_copy(ins[i], block(outs, i, shard), own_sem.at[i]) for i in range(6)]
    own.append(pltpu.make_async_copy(ins[SMALL], small_all.at[shard], own_sem.at[SMALL]))
    to_mate = [remote(ins[i], block(outs, i, shard), mate_send.at[i], mate_recv.at[i], mate) for i in range(6)]
    small_out = [
        remote(ins[SMALL], small_all.at[shard], small_send.at[d], small_recv.at[d], (rep, (shard + d) % shards))
        for d in range(1, shards)
    ]

    def small_wait(d):
        s = (shard - d + shards) % shards
        remote(small_all.at[s], small_all.at[s], small_send.at[d], small_recv.at[d], mate).wait_recv()

    WAYS = (0, 1)

    def source(way, t):
        return (pos - t if way == 0 else pos + t) * 2 + core

    def arrives(way, t):
        return pos - t >= 0 if way == 0 else pos + t < line

    def onward(way):
        return pos + 1 < line if way == 0 else pos > 0

    def line_copy(item, way, t):
        region = piece(outs, item, rep, source(way, t))
        at = (item, way * line + t)
        return remote(
            piece(ins, item, rep, 0) if t == 0 else region, region, line_send.at[at], line_recv.at[at],
            here.along(pos + 1 if way == 0 else pos - 1),
        )

    def take(item, way, t):
        region = piece(outs, item, rep, source(way, t))
        at = (item, way * line + t - 1)
        remote(region, region, line_send.at[at], line_recv.at[at], mate).wait_recv()
        if t + 1 < line:
            cond(onward(way), lambda: line_copy(item, way, t).start())

    def each_source(action):
        for t in range(1, line):
            for way in WAYS:
                cond(arrives(way, t), functools.partial(action, way, t))

    def hop(t):
        s = (pos - t) * 2 + core
        src = ins[HIDDEN] if t == 0 else block(outs, HIDDEN, s)
        return remote(
            src, block(outs, HIDDEN, s), line_send.at[HIDDEN, t], line_recv.at[HIDDEN, t], here.along(pos + 1)
        )

    def hop_wait(t):
        region = block(outs, HIDDEN, (pos - t) * 2 + core)
        remote(region, region, line_send.at[HIDDEN, t - 1], line_recv.at[HIDDEN, t - 1], mate).wait_recv()

    def far(item, at, s):
        return remote(block(outs, item, s), block(outs, item, s), far_send.at[item, at], far_recv.at[item, at], mate)

    def mate_block(s):
        return s + 1 - 2 * core

    def relay(t):
        def arrived():
            hop_wait(t)
            if t + 1 < line:
                cond(pos + 1 < line, lambda: hop(t).start())
            far(HIDDEN, t, (pos - t) * 2 + core).start()

        cond(pos - t >= 0, arrived)

    def relay_wait(t):
        far(HIDDEN, t, (pos - t) * 2 + 1 - core).wait_recv()

    def rep_at(step, more):
        return (1 << step) - 1 + subsets(range(step)).index(more)

    def rep_copy(item, way, t, step, more):
        region = piece(outs, item, here.subset(rep, more), source(way, t))
        at = (item, way * line + t, rep_at(step, more))
        return remote(region, region, rep_send.at[at], rep_recv.at[at], (here.flipped(rep, step), shard))

    def rep_wait(item, way, t, step, more):
        region = piece(outs, item, here.subset(here.flipped(rep, step), more), source(way, t))
        at = (item, way * line + t, rep_at(step, more))
        remote(region, region, rep_send.at[at], rep_recv.at[at], mate).wait_recv()

    def spread(item, step):
        def one(way, t):
            if step == 0:
                take(item, way, t)
            else:
                for more in subsets(range(step - 1)):
                    rep_wait(item, way, t, step - 1, more)
            if step < bits:
                for more in subsets(range(step)):
                    rep_copy(item, way, t, step, more).start()
            else:
                far(item, way * line + t, source(way, t)).start()

        each_source(one)

    def pass_on(item):
        def one(way, t):
            take(item, way, t)
            far(item, way * line + t, source(way, t)).start()

        each_source(one)

    def complete(item):
        own[item].wait()
        to_mate[item].wait_recv()
        each_source(lambda way, t: far(item, way * line + t, mate_block(source(way, t))).wait_recv())


    own[SMALL].start()
    for copy in small_out:
        copy.start()
    for i in (SELF, HIDDEN, CROSS, FC_IN, FC_OUT, ENCODED):
        to_mate[i].start()
        own[i].start()

    def send(item):
        for way in WAYS:
            cond(onward(way), lambda: line_copy(item, way, 0).start())

    send(SELF)
    cond(pos + 1 < line, lambda: hop(0).start())
    for item in (CROSS, FC_IN, FC_OUT, ENCODED):
        send(item)


    pairs = width // 128
    scale = 64 ** (-0.5)
    own_rows = pl.ds(pl.multiple_of(shard * rows, rows), rows)

    def block_of(b):
        return pl.ds(pl.multiple_of(b * rows, rows), rows)

    def gain(i):
        return params[11 + i : 12 + i, :]

    def shift(i):
        return params[14 + i : 15 + i, :]

    def write_k(b, slot):
        return pltpu.make_async_copy(kbuf.at[slot], keys.at[block_of(b)], k_sem.at[slot])

    def write_v(b, slot):
        return pltpu.make_async_copy(vbuf.at[slot], values.at[block_of(b)], v_sem.at[slot])

    count = segs.shape[1]
    ids = lax.broadcasted_iota(jnp.int32, (128, rows), 0)
    for b in range(count // rows):
        at = slice(b * rows, (b + 1) * rows)
        hot[at, :] = jnp.transpose((ids == segs[:, at]).astype(F32)).astype(BF)
    link = parents[...]
    line_ = lax.broadcasted_iota(jnp.int32, (128, 128), 0)
    across_ = lax.broadcasted_iota(jnp.int32, (128, 128), 1)
    reach = jnp.where(line_ == across_, 1.0, 0.0) + link.astype(F32) + nn(link, link)
    seen = nn(hot[own_rows, :], reach.astype(BF))
    hide = jnp.where(seen > 0.5, 0.0, NEGATIVE).astype(BF)
    hide = jnp.concatenate([hide, hide], axis=0)
    attend_start(top, total, acc)
    sums[...] = jnp.zeros_like(sums)
    grad_n2[...] = jnp.zeros_like(grad_n2)

    own[SMALL].wait()
    for d in range(1, shards):
        small_wait(d)
    part = width // shards
    for s in range(shards):
        some = small_all[s].astype(F32)
        params[:, s * part : (s + 1) * part] = some[:, :part]
        for u in range(UNITS):
            at = s * part * UNITS + u * part
            bias_in[:, at : at + part] = some[7 + u : 8 + u, :part]

    def norm0(values_):
        hat, _ = normalise(values_.astype(F32))
        return (hat * gain(0) + shift(0)).astype(BF)

    spread(SELF, 0)
    own[HIDDEN].wait()
    held[...] = norm0(hidden[own_rows, :])
    for step in range(1, bits):
        spread(SELF, step)
    relay(1)
    spread(CROSS, 0)
    spread(SELF, bits)
    to_mate[HIDDEN].wait_recv()
    complete(SELF)

    q = ((nn(held[...], w_self[0]) + params[0:1, :]).astype(BF) * scale).astype(BF)
    for pair in range(pairs):
        queries[pair, :, 0:128] = pair_rows(q, pair)
        queries[pair, :, 128:256] = hide

    def one_block(b, j, diagonal):
        slot = j % 2
        norm = held[...] if diagonal else norm0(hidden[block_of(b), :])

        @pl.when(j >= 2)
        def _():
            write_k(b, slot).wait()
            write_v(b, slot).wait()

        kbuf[slot] = nn(norm, w_self[1]).astype(BF)
        v = (nn(norm, w_self[2]) + params[1:2, :]).astype(BF)
        vbuf[slot] = v
        turned[...] = jnp.transpose(v)
        write_k(b, slot).start()
        write_v(b, slot).start()
        attend_block(queries, kbuf.at[slot], turned, hot[block_of(b), :], top, total, acc, diagonal)

    one_block(shard, jnp.int32(0), True)

    duties = {}

    def duty(j, action, *args):
        duties.setdefault(j, []).append(functools.partial(action, *args))

    last = shards - 1
    for t in range(2, line):
        duty(2 * t - 3, relay, t)
    duty(2, spread, CROSS, 1)
    duty(2, spread, FC_IN, 0)
    for step in range(2, bits + 1):
        duty(4, spread, CROSS, step)
    duty(4, spread, FC_IN, 1)
    duty(4, spread, FC_OUT, 0)
    duty(5, pass_on, ENCODED)
    for step in range(2, bits + 1):
        duty(6, spread, FC_IN, step)
    duty(7, spread, FC_OUT, 1)

    def step_block(j, carry):
        b = shard - j
        for when_, actions in sorted(duties.items()):
            @pl.when(j == when_)
            def _(actions=actions):
                for action in actions:
                    action()

        for t in range(1, line):
            @pl.when(jnp.logical_and(b >= 0, j == 2 * t - 1 + core))
            def _(t=t):
                relay_wait(t)

        @pl.when(b >= 0)
        def _():
            one_block(b, j, False)

        return carry

    lax.fori_loop(1, shards, step_block, 0)
    attend_finish(top, total, acc, lse, att)
    after_self[...] = hidden[own_rows, :].astype(F32) + nn(att[...].astype(BF), w_self[3]) + params[4:5, :]
    hat1, _ = normalise(after_self[...])
    normed1[...] = (hat1 * gain(1) + shift(1)).astype(BF)
    keep = [
        pltpu.make_async_copy(w_self, keep_self, keep_sem.at[0]),
        pltpu.make_async_copy(w_cross, keep_cross, keep_sem.at[1]),
        pltpu.make_async_copy(states, keep_states, keep_sem.at[2]),
        pltpu.make_async_copy(hidden.at[own_rows], keep_hidden.at[own_rows], keep_sem.at[3]),
    ]
    keep[0].start()
    keep[3].start()

    def keep_block(b):
        return pltpu.make_async_copy(hidden.at[block_of(b)], keep_hidden.at[block_of(b)], keep_sem.at[4 + b])

    for b in range(shards):
        cond(b < shard, lambda: keep_block(b).start())

    complete(CROSS)
    keep[1].start()
    cq = ((nn(normed1[...], w_cross[0]) + params[2:3, :]).astype(BF) * scale).astype(BF)
    for pair in range(pairs):
        c_queries[pair] = pair_rows(cq, pair)
    attend_start(top, total, acc)
    complete(ENCODED)
    keep[2].start()

    def c_block(b, carry):
        at = block_of(b)
        c_keys[at, :] = nn(states[at, :], w_cross[1]).astype(BF)
        v = (nn(states[at, :], w_cross[2]) + params[3:4, :]).astype(BF)
        c_values[at, :] = v
        c_turned[...] = jnp.transpose(v)
        attend_block(c_queries, c_keys.at[at], c_turned, None, top, total, acc, False)

        for step in range(2, bits + 1):
            @pl.when(b == min(step - 2, frames // rows - 1))
            def _(step=step):
                spread(FC_OUT, step)

        return carry

    lax.fori_loop(0, frames // rows, c_block, 0)
    attend_finish(top, total, acc, c_lse, catt)
    after_cross = after_self[...] + nn(catt[...].astype(BF), w_cross[3]) + params[5:6, :]
    hat2, scale2 = normalise(after_cross)
    normed2 = (hat2 * gain(2) + shift(2)).astype(BF)
    held[...] = normed2
    result[...] = after_cross + params[6:7, :]
    turned2 = jnp.transpose(normed2)
    each = gbuf_out.shape[1]
    complete(FC_IN)
    complete(FC_OUT)

    def send_grads(u):
        return (
            pltpu.make_async_copy(gbuf_out.at[u % 2], grads.at[0, pl.ds(u * each, each)], g_sem.at[0, u % 2]),
            pltpu.make_async_copy(gbuf_in.at[u % 2], grads.at[1, :, :, pl.ds(u * part, part)], g_sem.at[1, u % 2]),
        )

    for u in range(UNITS):
        at = slice(u * width, (u + 1) * width)
        norm2 = held[...]
        pre = nn(norm2, w_in[:, at]) + bias_in[:, at]
        cdf, slope = erf_parts(pre)
        act = (pre * cdf).astype(BF)
        result[...] += nn(act, w_out[at, :])
        grad_pre = (slope * nt(cotangent[...], w_out[at, :])).astype(BF)
        grad_n2[...] += nt(grad_pre, w_in[:, at])
        if u >= 2:
            for copy in send_grads(u - 2):
                copy.wait()
        g = nn(turned2, grad_pre)
        for s in range(shards):
            gbuf_in[u % 2, s // 2, s % 2] = g[s * part : (s + 1) * part].astype(BF)
        g = nn(jnp.transpose(act), cotangent[...])
        tall = part * UNITS
        for j in range(width // tall):
            gbuf_out[u % 2, j // 2, j % 2] = g[j * tall : (j + 1) * tall].astype(BF)
        for copy in send_grads(u):
            copy.start()
        sums[V_IN + u : V_IN + u + 1, :] = column_sums(grad_pre.astype(F32))

    grad = cotangent[...].astype(F32)
    dn = grad_n2[...]
    grad_across[...] = grad + norm_back(hat2, scale2, gain(2), dn)
    sums[V_OUT + 2 : V_OUT + 3, :] = column_sums(grad)
    sums[V_GAIN + 2 : V_GAIN + 3, :] = column_sums(dn * hat2)
    sums[V_SHIFT + 2 : V_SHIFT + 3, :] = column_sums(dn)

    for u in (UNITS - 2, UNITS - 1):
        for copy in send_grads(u):
            copy.wait()
    write_k(shard, shard % 2).wait()
    write_v(shard, shard % 2).wait()

    @pl.when(shard >= 1)
    def _():
        write_k(shard - 1, (shard + 1) % 2).wait()
        write_v(shard - 1, (shard + 1) % 2).wait()

    for copy in keep:
        copy.wait()
    for b in range(shards):
        cond(b < shard, lambda: keep_block(b).wait())
    for i in range(6):
        to_mate[i].wait_send()
    for copy in small_out:
        copy.wait_send()
    for item in WEIGHTS + (ENCODED,):
        for way in WAYS:
            cond(onward(way), lambda: line_copy(item, way, 0).wait_send())

        def drain(way, t):
            if t + 1 < line:
                cond(onward(way), lambda: line_copy(item, way, t).wait_send())
            far(item, way * line + t, source(way, t)).wait_send()
            if item in WEIGHTS:
                for step in range(bits):
                    for more in subsets(range(step)):
                        rep_copy(item, way, t, step, more).wait_send()

        each_source(drain)
    cond(pos + 1 < line, lambda: hop(0).wait_send())
    for t in range(1, line):
        def drain_tokens():
            if t + 1 < line:
                cond(pos + 1 < line, lambda: hop(t).wait_send())
            far(HIDDEN, t, (pos - t) * 2 + core).wait_send()

        cond(pos - t >= 0, drain_tokens)


def forward(mesh_shape, self4, cross4, fc_in, fc_out, hidden, encoded, small, segs, parents, cotangent):
    shards, reps = mesh_shape
    line, bits = shards // 2, reps.bit_length() - 1
    rows, width = cotangent.shape
    count, frames = rows * shards, encoded.shape[0] * shards
    pairs = width // 128
    unit_rows = fc_out.shape[0]
    part = width // shards
    each = width // unit_rows // 2
    f32, bf = functools.partial(shape_of, F32), functools.partial(shape_of, BF)
    vm, hbm = pl.BlockSpec(memory_space=pltpu.VMEM), pl.BlockSpec(memory_space=pl.ANY)
    dma = pltpu.SemaphoreType.DMA

    def bv(*shape):
        return pltpu.VMEM(shape, BF)

    def fv(*shape):
        return pltpu.VMEM(shape, F32)

    return pl.pallas_call(
        functools.partial(forward_kernel, shards, reps),
        out_shape=(
            f32(rows, width), f32(rows, width), bf(2, line, 2, unit_rows, width), bf(count, width),
            bf(count, width), bf(pairs, 2 * rows, 256), bf(count, 128), f32(8, 2 * rows), f32(rows, width),
            bf(pairs, 2 * rows, 128), bf(frames, width), bf(frames, width), f32(8, 2 * rows),
            f32(rows, width), f32(rows, width), bf(rows, width), f32(GRAD_ROWS, width), f32(SMALL_ROWS, width),
            bf(UNITS, width, width), bf(UNITS, width, width), bf(count, width), bf(frames, width),
        ),
        in_specs=[hbm] * 7 + [vm] * 3,
        out_specs=[vm, vm, hbm, hbm, hbm] + [vm] * 13 + [hbm] * 4,
        scratch_shapes=[
            bv(UNITS, width, width), bv(UNITS, width, width), bv(width, UNITS * width), bv(UNITS * width, width),
            bv(count, width), bv(frames, width), bv(shards, SMALL_ROWS, 128), fv(1, UNITS * width),
            bv(2, rows, width), bv(2, rows, width), bv(width, rows), bv(width, rows),
            fv(8, 2 * rows), fv(8, 2 * rows), fv(pairs, 128, 2 * rows), fv(rows, width), bv(rows, width),
            bv(2, line, 2, part, width), bv(2, each, 2, unit_rows, width),
            dma((2,)), dma((2,)), dma((2, 2)), dma((4 + shards,)), dma((7,)), dma((7,)), dma((7,)),
            dma((6, 2 * line)), dma((6, 2 * line)), dma((4, 2 * line, reps)), dma((4, 2 * line, reps)),
            dma((6, 2 * line)), dma((6, 2 * line)), dma((shards,)), dma((shards,)),
        ],
        compiler_params=pltpu.CompilerParams(
            collective_id=0, has_side_effects=True, vmem_limit_bytes=60 * 2**20
        ),
        name="forward",
    )(self4, cross4, fc_in, fc_out, hidden, encoded, small, segs, parents, cotangent)


def backward_kernel(shards, reps, *refs):
    (ffn, hidden, states, keys, values, c_keys, c_values, keep_self, keep_cross) = refs[:9]
    (params, grad_across, queries, hot, lse, att, c_queries, c_lse, catt, after_self, normed1, sums_in) = refs[9:21]
    (d_hidden, out_denc, out_small, out, got_mate, got_rep, x_mate, x_line) = refs[21:29]
    (weights, mine, accf, stage, got_line, shared, finish, x_own, x_send, d_states, e_mate, e_own, e_line,
     s_src, s_line, s_rep, sums, dn_own, grad_after_self,
     hbuf, kbuf, vbuf, turned, pair_grads, delta, grad_q, grad_k, grad_v, gk_acc, gv_acc,
     r_sem, w_sem, load_sem, stage_sem, out_sem, mate_send, mate_recv, rep_send, rep_recv, line_send, line_recv,
     share_send, share_recv, xm_send, xm_recv, xl_send, xl_recv, em_send, em_recv, el_send, el_recv,
     s_send, s_recv, t_send, t_recv) = refs[29:]
    here = Place(shards, reps)
    line, bits = here.line, here.bits
    pos, core, rep, shard = here.pos, here.core, here.rep, here.shard
    rows, width = grad_across.shape
    frames = states.shape[0]
    fr = frames // shards
    part = width // shards
    strip = width * UNITS // reps
    scale = 64 ** (-0.5)
    pairs = width // 128
    other = 1 - core
    mate = here.partner()

    halves = 2 if reps == UNITS and width % 256 == 0 else 1
    jobs = [(G_OUT, 0, strip), (G_IN, 0, strip), (G_CROSS, 0, strip)]
    jobs += [(G_SELF, h * (strip // halves), strip // halves) for h in range(halves)]

    greet(
        [(rep, (shard + d) % shards) for d in range(1, shards)]
        + [((rep + e) % reps, shard) for e in range(1, reps)],
        [None] * (shards + reps - 2),
    )

    def held(g):
        return accf.at[g] if g < 2 else mine.at[g - 2, :, core]

    def leaving(g):
        return ffn.at[g, :, other] if g < 2 else mine.at[g - 2, :, other]

    def span(job):
        g, at, size = jobs[job]
        return pl.ds(0, width) if reps != UNITS else pl.ds(at, size)

    def swap(job):
        g = jobs[job][0]
        return remote(
            leaving(g).at[:, :, span(job)], got_mate.at[g, :, :, span(job)], mate_send.at[job], mate_recv.at[job], mate
        )

    def columns(r, job):
        g, at, size = jobs[job]
        if reps == UNITS:
            return pl.ds(at, size)
        return pl.ds(pl.multiple_of((r // UNITS) * strip + at, 128), size)

    def piece(job, r):
        return held(jobs[job][0]).at[:, pl.ds(pl.multiple_of((r % UNITS) * part, 16), part), columns(r, job)]

    def plus(a, b):
        return (a.astype(F32) + b.astype(F32)).astype(BF)

    def add_all(into, other_ref):
        def add(i, carry):
            into[i] = plus(into[i], other_ref[i])
            return carry

        lax.fori_loop(0, line, add, 0)

    load = [pltpu.make_async_copy(ffn.at[g, :, core], accf.at[g], load_sem.at[g]) for g in range(2)]

    def rep_copy(job, step, more):
        g, at, size = jobs[job]
        slot = (1 << bits) - (1 << (bits - step)) + subsets(range(step + 1, bits)).index(more)
        target = here.flipped(rep, step)
        return remote(
            piece(job, here.subset(target, more)), got_rep.at[g, slot, :, :, pl.ds(at, size)],
            rep_send.at[job, slot], rep_recv.at[job, slot], (target, shard),
        ), slot

    def send_rep(job, step):
        for more in subsets(range(step + 1, bits)):
            rep_copy(job, step, more)[0].start()

    def line_copy(job, d):
        g, at, size = jobs[job]
        to = (pos + d) % line
        return remote(
            piece(job, rep).at[to], got_line.at[g, d, :, pl.ds(at, size)], line_send.at[job, d], line_recv.at[job, d],
            here.along(to),
        )

    def share_copy(job, e):
        g, at, size = jobs[job]
        own = shared.at[g, rep, :, pl.ds(at, size)]
        return remote(own, own, share_send.at[job, e], share_recv.at[job, e], ((rep + e) % reps, shard))

    def share_wait(job, e):
        g, at, size = jobs[job]
        got = shared.at[g, (rep - e + reps) % reps, :, pl.ds(at, size)]
        remote(got, got, share_send.at[job, e], share_recv.at[job, e], ((rep + e) % reps, shard)).wait_recv()

    def stage_mate(job):
        g = jobs[job][0]
        if g < 2:
            load[g].wait()
        swap(job).wait()
        staged = stage.at[:, :, span(job)]
        copy = pltpu.make_async_copy(got_mate.at[g, :, :, span(job)], staged, stage_sem.at[0])
        copy.start()
        copy.wait()
        add_all(held(g).at[:, :, span(job)], staged)
        send_rep(job, 0)

    def stage_rep(job, step):
        g, at, size = jobs[job]
        staged = []
        for i, more in enumerate(subsets(range(step + 1, bits))):
            copy, slot = rep_copy(job, step, more)
            copy.wait()
            into = stage.at[:, pl.ds((i % UNITS) * part, part), pl.ds((i // UNITS) * size, size)]
            staged.append((more, into, pltpu.make_async_copy(
                got_rep.at[g, slot, :, :, pl.ds(at, size)], into, stage_sem.at[i]
            )))
            staged[-1][2].start()
        for more, into, copy in staged:
            copy.wait()
            add_all(piece(job, here.subset(rep, more)), into)
        if step + 1 < bits:
            send_rep(job, step + 1)
        else:
            for d in range(1, line):
                line_copy(job, d).start()

    def stage_line(job):
        g, at, size = jobs[job]
        total = piece(job, rep)[pos].astype(F32)
        for d in range(1, line):
            line_copy(job, d).wait()
            total = total + got_line[g, d, :, at : at + size].astype(F32)
        shared[g, rep, :, at : at + size] = total.astype(BF)
        for e in range(1, reps):
            share_copy(job, e).start()

    def out_copy(job):
        g = jobs[job][0]
        return pltpu.make_async_copy(finish.at[job % 2, :, span(job)], out.at[g, :, span(job)], out_sem.at[job])

    def stage_share(job):
        g, at, size = jobs[job]
        for e in range(1, reps):
            share_copy(job, e).wait_send()
            share_wait(job, e)
        if job >= 2:
            out_copy(job - 2).wait()
        for r in range(reps):
            unit, first = r % UNITS, (r // UNITS) * strip + at
            finish[job % 2, unit * part : (unit + 1) * part, first : first + size] = (
                shared[g, r, :, at : at + size].astype(F32)
            )
        out_copy(job).start()


    def x_swap(at):
        return remote(x_send.at[at], x_mate.at[at], xm_send.at[at], xm_recv.at[at], mate)

    def x_down(t):
        return remote(x_own.at[pos - t], x_line.at[t - 1], xl_send.at[t], xl_recv.at[t - 1], here.along(pos - 1))

    def x_flush(t):
        def flush():
            at = pos - t
            x_swap(at).wait()
            copy = pltpu.make_async_copy(x_mate.at[at], hbuf.at[2], stage_sem.at[0])
            copy.start()
            copy.wait()
            x_own[at] = plus(x_own[at], hbuf[2])

        cond(pos - t >= 0, flush)

    def x_chain(t):
        def link_():
            def take():
                remote(x_line.at[t], x_line.at[t], xl_send.at[t], xl_recv.at[t], mate).wait_recv()
                copy = pltpu.make_async_copy(x_line.at[t], hbuf.at[2], stage_sem.at[0])
                copy.start()
                copy.wait()
                x_own[pos - t] = plus(x_own[pos - t], hbuf[2])

            if t + 1 < line:
                cond(pos + 1 < line, take)
            if t > 0:
                x_down(t).start()

        cond(pos - t >= 0, link_)

    top_end = pos == line - 1


    def e_swap(i):
        return remote(
            d_states.at[pl.ds(pl.multiple_of((2 * i + other) * fr, 16), fr)], e_mate.at[i], em_send.at[i], em_recv.at[i],
            mate,
        )

    def e_out(d):
        to = (pos + d) % line
        return remote(e_own.at[to], e_line.at[d], el_send.at[d], el_recv.at[d], here.along(to))

    def e_stage():
        for i in range(line):
            e_swap(i).wait()
            mine_rows = d_states[pl.ds(pl.multiple_of((2 * i + core) * fr, 16), fr), :]
            e_own[i] = plus(mine_rows, e_mate[i])
        for d in range(1, line):
            e_out(d).start()

    def e_finish():
        total = e_own[pos].astype(F32)
        for d in range(1, line):
            e_out(d).wait()
            total = total + e_line[d].astype(F32)
        out_denc[...] = total


    def s_out(d):
        to = (shard + d) % shards
        return remote(s_src.at[to], s_line.at[d], s_send.at[d], s_recv.at[d], (rep, to))

    def s_share(e):
        return remote(s_rep.at[rep], s_rep.at[rep], t_send.at[e], t_recv.at[e], ((rep + e) % reps, shard))

    def s_start():
        for s in range(shards):
            s_src[s, 0:13, 0:part] = sums[0:13, s * part : (s + 1) * part]
            for u in range(UNITS):
                at = (s * UNITS + u) * part
                row = V_IN + at // width
                s_src[s, V_IN + u : V_IN + u + 1, 0:part] = sums[row : row + 1, at % width : at % width + part]
        for d in range(1, shards):
            s_out(d).start()

    def s_middle():
        total = s_src[shard]
        for d in range(1, shards):
            s_out(d).wait()
            total = total + s_line[d]
        s_rep[rep] = total
        for e in range(1, reps):
            s_share(e).start()

    def s_finish():
        for e in range(1, reps):
            s_share(e).wait_send()
            got = s_rep.at[(rep - e + reps) % reps]
            remote(got, got, t_send.at[e], t_recv.at[e], ((rep + e) % reps, shard)).wait_recv()
        total = s_rep[0]
        for r in range(1, reps):
            total = total + s_rep[r]
        out_small[...] = total


    for g in range(2):
        swap(g).start()
        load[g].start()

    def block_of(b):
        return pl.ds(pl.multiple_of(b * rows, rows), rows)

    def reads(cross, b, slot):
        sources = (states, c_keys, c_values) if cross else (hidden, keys, values)
        return [
            pltpu.make_async_copy(src.at[block_of(b)], buf.at[slot], r_sem.at[i, slot])
            for i, (src, buf) in enumerate(zip(sources, (hbuf, kbuf, vbuf)))
        ]

    def weight(source, unit):
        return pltpu.make_async_copy(source.at[unit], weights.at[unit], w_sem.at[unit])

    for unit in (3, 1, 2, 0):
        weight(keep_cross, unit).start()
    for copy in reads(True, 0, 0):
        copy.start()

    def gain(i):
        return params[11 + i : 12 + i, :]

    s_src[...] = jnp.zeros_like(s_src)
    sums[...] = sums_in[...]
    grad = grad_across[...]
    branch = grad.astype(BF)
    sums[V_OUT + 1 : V_OUT + 2, :] = column_sums(branch.astype(F32))
    store_owners(mine, 0, 3, nn(jnp.transpose(catt[...].astype(BF)), branch), shards)
    weight(keep_cross, 3).wait()
    g_catt = nt(branch, weights[3]).astype(BF)
    weight(keep_self, 3).start()
    deltas(g_catt, catt[...], delta, pairs)
    for pair in range(pairs):
        pair_grads[pair] = pair_rows(g_catt, pair)
    grad_q[...] = jnp.zeros_like(grad_q)
    gk_acc[...] = jnp.zeros_like(gk_acc)
    gv_acc[...] = jnp.zeros_like(gv_acc)
    sums[V_PROJ + 3 : V_PROJ + 4, :] = jnp.zeros((1, width), F32)
    stage_mate(0)
    weight(keep_cross, 1).wait()
    weight(keep_cross, 2).wait()
    c_blocks = frames // rows

    def c_block(b, carry):
        slot = b % 2
        for copy in reads(True, b, slot):
            copy.wait()

        @pl.when(b + 1 < c_blocks)
        def _():
            for copy in reads(True, b + 1, 1 - slot):
                copy.start()

        turned[...] = jnp.transpose(kbuf[slot])
        attend_back_block(
            c_queries, pair_grads, kbuf.at[slot], vbuf.at[slot], turned, None, c_lse, delta, grad_q, grad_k, grad_v, False
        )
        gk, gv = grad_k[...], grad_v[...]
        flipped = jnp.transpose(hbuf[slot])
        gk_acc[...] += nn(flipped, gk)
        gv_acc[...] += nn(flipped, gv)
        d_states[block_of(b), :] = (nt(gk, weights[1]) + nt(gv, weights[2])).astype(BF)
        sums[V_PROJ + 3 : V_PROJ + 4, :] += column_sums(gv.astype(F32))

        @pl.when(b == 0)
        def _():
            stage_mate(1)

        return carry

    lax.fori_loop(0, c_blocks, c_block, 0)
    for unit in (1, 2):
        weight(keep_self, unit).start()
    for copy in reads(False, shard, 0):
        copy.start()
    for i in range(line):
        e_swap(i).start()
    store_owners(mine, 0, 1, gk_acc[...], shards)
    store_owners(mine, 0, 2, gv_acc[...], shards)
    gcq = jnp.concatenate([(unpair(grad_q[pair]) * scale).astype(BF) for pair in range(pairs)], axis=1)
    sums[V_PROJ + 2 : V_PROJ + 3, :] = column_sums(gcq.astype(F32))
    store_owners(mine, 0, 0, nn(jnp.transpose(normed1[...]), gcq), shards)
    swap(2).start()
    weight(keep_cross, 0).wait()
    dn1 = nt(gcq, weights[0])
    weight(keep_self, 0).start()
    hat1, scale1 = normalise(after_self[...])
    sums[V_GAIN + 1 : V_GAIN + 2, :] = column_sums(dn1 * hat1)
    sums[V_SHIFT + 1 : V_SHIFT + 2, :] = column_sums(dn1)
    grad_after_self[...] = grad + norm_back(hat1, scale1, gain(1), dn1)
    stage_rep(0, 0)

    self_branch = grad_after_self[...].astype(BF)
    sums[V_OUT : V_OUT + 1, :] = column_sums(self_branch.astype(F32))
    store_owners(mine, 1, 3, nn(jnp.transpose(att[...].astype(BF)), self_branch), shards)
    weight(keep_self, 3).wait()
    g_att = nt(self_branch, weights[3]).astype(BF)
    deltas(g_att, att[...], delta, pairs)
    for pair in range(pairs):
        pair_grads[pair] = pair_rows(g_att, pair)
    grad_q[...] = jnp.zeros_like(grad_q)
    gk_acc[...] = jnp.zeros_like(gk_acc)
    gv_acc[...] = jnp.zeros_like(gv_acc)
    sums[V_PROJ + 1 : V_PROJ + 2, :] = jnp.zeros((1, width), F32)
    sums[V_GAIN : V_GAIN + 1, :] = jnp.zeros((1, width), F32)
    sums[V_SHIFT : V_SHIFT + 1, :] = jnp.zeros((1, width), F32)
    weight(keep_self, 1).wait()
    weight(keep_self, 2).wait()

    def one_block(b, j, diagonal):
        slot = j % 2
        for copy in reads(False, b, slot):
            copy.wait()

        @pl.when(b >= 1)
        def _():
            for copy in reads(False, b - 1, 1 - slot):
                copy.start()

        turned[...] = jnp.transpose(kbuf[slot])
        attend_back_block(
            queries, pair_grads, kbuf.at[slot], vbuf.at[slot], turned, hot[block_of(b), :], lse, delta,
            grad_q, grad_k, grad_v, diagonal,
        )
        hat, _ = normalise(hbuf[slot].astype(F32))
        norm = (hat * gain(0) + params[14:15, :]).astype(BF)
        gk, gv = grad_k[...], grad_v[...]
        flipped = jnp.transpose(norm)
        gk_acc[...] += nn(flipped, gk)
        gv_acc[...] += nn(flipped, gv)
        dn = nt(gk, weights[1]) + nt(gv, weights[2])

        @pl.when(b % 2 == core)
        def _():
            x_own[b // 2] = dn.astype(BF)

        @pl.when(b % 2 != core)
        def _():
            x_send[b // 2] = dn.astype(BF)
            x_swap(b // 2).start()

        sums[V_PROJ + 1 : V_PROJ + 2, :] += column_sums(gv.astype(F32))
        sums[V_GAIN : V_GAIN + 1, :] += column_sums(dn * hat)
        sums[V_SHIFT : V_SHIFT + 1, :] += column_sums(dn)

    one_block(shard, jnp.int32(0), True)

    @pl.when(core == 0)
    def _():
        x_send[pos] = jnp.zeros((rows, width), BF)
        x_swap(pos).start()

    stage_mate(2)
    duties = {}

    def duty(j, action, *args):
        duties.setdefault(max(1, min(j, shards - 1)), []).append(functools.partial(action, *args))

    last = shards - 1
    duty(2, stage_rep, 1, 0)
    for t in range(0, line - 1):
        duty(2 * t + 2, x_flush, t)
        if t > 0:
            duty(2 * t + 2, cond, top_end, functools.partial(x_chain, t))
    duty(3, e_stage)
    for step in range(1, bits):
        duty(1 + 2 * step, stage_rep, 0, step)
        duty(4 + 2 * step, stage_rep, 1, step)

    def step_block(j, carry):
        b = shard - j
        for when_, actions in sorted(duties.items()):
            @pl.when(j == when_)
            def _(actions=actions):
                for action in actions:
                    action()

        @pl.when(b >= 0)
        def _():
            one_block(b, j, False)

        return carry

    lax.fori_loop(1, shards, step_block, 0)
    store_owners(mine, 1, 1, gk_acc[...], shards)
    store_owners(mine, 1, 2, gv_acc[...], shards)
    gq = jnp.concatenate([(unpair(grad_q[pair]) * scale).astype(BF) for pair in range(pairs)], axis=1)
    sums[V_PROJ : V_PROJ + 1, :] = column_sums(gq.astype(F32))
    own_hidden = pltpu.make_async_copy(hidden.at[block_of(shard)], hbuf.at[0], r_sem.at[0, 0])
    own_hidden.start()
    own_hidden.wait()
    hat0, scale0 = normalise(hbuf[0].astype(F32))
    norm = (hat0 * gain(0) + params[14:15, :]).astype(BF)
    store_owners(mine, 1, 0, nn(jnp.transpose(norm), gq), shards)
    first_self = 3
    for job in range(first_self, len(jobs)):
        swap(job).start()
    weight(keep_self, 0).wait()
    dn = nt(gq, weights[0])
    dn_own[...] = dn
    sums[V_GAIN : V_GAIN + 1, :] += column_sums(dn * hat0)
    sums[V_SHIFT : V_SHIFT + 1, :] += column_sums(dn)
    s_start()
    selves = range(first_self, len(jobs))
    stage_rep(2, 0)
    for job in selves:
        stage_mate(job)
    x_flush(line - 1)
    cond(top_end, lambda: x_chain(line - 1))
    stage_line(0)
    stage_line(1)
    for step in range(1, bits):
        stage_rep(2, step)
    s_middle()
    for step in range(bits):
        for job in selves:
            stage_rep(job, step)
            if step == 0 and job == first_self:
                for t in range(1, line - 1):
                    cond(pos < line - 1, lambda: x_chain(t))
                stage_share(0)
    stage_line(2)
    stage_share(1)
    s_finish()
    e_finish()
    x_chain(0)
    for job in selves:
        stage_line(job)

    for t in range(1, line):
        cond(pos - t >= 0, lambda: x_down(t).wait_send())
    d_hidden[...] = dn_own[...] + x_own[pos].astype(F32)
    d_hidden[...] = grad_after_self[...] + norm_back(hat0, scale0, gain(0), d_hidden[...])
    stage_share(2)
    for job in selves:
        stage_share(job)
    for job in range(len(jobs) - 2, len(jobs)):
        out_copy(job).wait()


def backward(mesh_shape, ffn, hidden, states, keys, values, c_keys, c_values, keep_self, keep_cross, *saved):
    shards, reps = mesh_shape
    line, bits = shards // 2, reps.bit_length() - 1
    rows, width = saved[1].shape
    frames = states.shape[0]
    fr = frames // shards
    pairs = width // 128
    part = width // shards
    unit_rows = UNITS * part
    strip = width * UNITS // reps
    f32, bf = functools.partial(shape_of, F32), functools.partial(shape_of, BF)
    vm, hbm = pl.BlockSpec(memory_space=pltpu.VMEM), pl.BlockSpec(memory_space=pl.ANY)
    dma = pltpu.SemaphoreType.DMA
    most = 5

    def bv(*shape):
        return pltpu.VMEM(shape, BF)

    def fv(*shape):
        return pltpu.VMEM(shape, F32)

    return pl.pallas_call(
        functools.partial(backward_kernel, shards, reps),
        out_shape=(
            f32(rows, width), f32(fr, width), f32(GRAD_ROWS, 128), f32(4, unit_rows, width),
            bf(4, line, unit_rows, width), bf(4, reps, line, part, strip), bf(line, rows, width), bf(line, rows, width),
        ),
        in_specs=[hbm] * 9 + [vm] * 12,
        out_specs=[vm, vm, vm] + [hbm] * 5,
        scratch_shapes=[
            bv(UNITS, width, width), bv(2, line, 2, unit_rows, width), bv(2, line, unit_rows, width),
            bv(line, unit_rows, width), bv(4, line, part, strip), bv(4, reps, part, strip), fv(2, unit_rows, width),
            bv(line, rows, width), bv(line, rows, width), bv(frames, width), bv(line, fr, width), bv(line, fr, width),
            bv(line, fr, width), fv(shards, GRAD_ROWS, 128), fv(shards, GRAD_ROWS, 128), fv(reps, GRAD_ROWS, 128),
            fv(GRAD_ROWS, width), fv(rows, width), fv(rows, width),
            bv(3, rows, width), bv(2, rows, width), bv(2, rows, width), bv(width, rows),
            bv(pairs, 2 * rows, 128), fv(8, 2 * rows), fv(pairs, 128, 2 * rows), bv(rows, width), bv(rows, width),
            fv(width, width), fv(width, width),
            dma((3, 2)), dma((UNITS,)), dma((2,)), dma((max(reps, 2),)), dma((most,)), dma((most,)), dma((most,)),
            dma((most, reps)), dma((most, reps)), dma((most, line)), dma((most, line)), dma((most, reps)), dma((most, reps)),
            dma((line,)), dma((line,)), dma((line,)), dma((line,)), dma((line,)), dma((line,)), dma((line,)), dma((line,)),
            dma((shards,)), dma((shards,)), dma((reps,)), dma((reps,)),
        ],
        compiler_params=pltpu.CompilerParams(
            collective_id=1, has_side_effects=True, vmem_limit_bytes=62 * 2**20
        ),
        name="backward",
    )(ffn, hidden, states, keys, values, c_keys, c_values, keep_self, keep_cross, *saved)


def local(
    shards, reps, hidden, encoded, tok_seg, seg_parent, self_qkv, self_out, cross_qkv, cross_out,
    fc_in, fc_out, proj_bias, out_bias, fc_in_bias, norm_gain, norm_bias, cotangent,
):
    rows, width = hidden.shape
    strip = norm_gain.shape[1]
    small = jnp.concatenate(
        [proj_bias, out_bias, fc_in_bias.reshape(UNITS, strip), norm_gain, norm_bias], axis=0
    )
    small = jnp.pad(small, ((0, SMALL_ROWS - small.shape[0]), (0, 128 - strip)))
    ids = jnp.arange(128, dtype=jnp.int32)
    parents = jnp.pad(seg_parent[0], (0, 128 - seg_parent.shape[1]), constant_values=-1)
    parents = (parents[:, None] == ids[None, :]).astype(BF)

    (result, grad_across, ffn, keys, values, queries, hot, lse, att, c_queries, c_keys, c_values, c_lse, catt,
     after_self, normed1, sums, params, w_self, w_cross, all_hidden, states) = forward(
        (shards, reps), jnp.concatenate([self_qkv, self_out[None]]), jnp.concatenate([cross_qkv, cross_out[None]]),
        fc_in, fc_out, hidden, encoded, small, tok_seg, parents, cotangent,
    )
    d_hidden, d_encoded, vector_sum, total = backward(
        (shards, reps), ffn, all_hidden, states, keys, values, c_keys, c_values, w_self, w_cross,
        params, grad_across, queries, hot, lse, att, c_queries, c_lse, catt, after_self, normed1, sums,
    )[:4]
    vector_sum = vector_sum[:, :strip]
    by_unit = total.reshape(4, UNITS, strip, width)
    return (
        result, d_hidden, d_encoded,
        by_unit[3, :3], by_unit[3, 3], by_unit[2, :3], by_unit[2, 3],
        jnp.transpose(by_unit[1], (1, 0, 2)).reshape(strip, UNITS * width), total[0],
        vector_sum[0:4], vector_sum[4:7], vector_sum[13:17].reshape(UNITS * strip),
        vector_sum[7:10], vector_sum[10:13],
    )


def solution(mesh):
    across = P(("rep", "shard"), None)
    matrix, matrices, vectors = P("shard", None), P(None, "shard", None), P(None, "shard")
    return jax.shard_map(
        functools.partial(local, mesh.shape["shard"], mesh.shape["rep"]),
        mesh=mesh,
        in_specs=(
            across, across, P("rep", None), P("rep", None), matrices, matrix, matrices, matrix, matrix, matrix,
            vectors, vectors, P("shard"), vectors, vectors, across,
        ),
        out_specs=(
            across, across, across, matrices, matrix, matrices, matrix, matrix, matrix,
            vectors, vectors, P("shard"), vectors, vectors,
        ),
        check_vma=False,
    )
```

```python
import functools
import math

import jax
import jax.numpy as jnp
from jax import lax
from jax.experimental import pallas as pl
from jax.experimental.pallas import tpu as pltpu
from jax.sharding import PartitionSpec as P

HEADS = 12
EPS = 1e-05
NEGATIVE = -1e30
MESH = pl.DeviceIdType.MESH
UNITS = 4
SMALL_ROWS = 32
GRAD_ROWS = 24
BF = jnp.bfloat16
F32 = jnp.float32


def flip_bit(index, bit):
    size = 1 << bit
    return index + size * (1 - 2 * ((index // size) % 2))


def pick(core, first, second):
    return first + core * (second - first)


class Place:
    def __init__(self, shards, reps):
        self.shards, self.reps = shards, reps
        self.rep = lax.axis_index("rep")
        self.shard = lax.axis_index("shard")
        self.pos = self.shard // 2
        self.core = self.shard % 2
        self.line = shards // 2
        self.bits = reps.bit_length() - 1

    def partner(self):
        return (self.rep, self.shard + 1 - 2 * self.core)

    def along(self, pos):
        return (self.rep, pos * 2 + self.core)

    def flipped(self, index, step):
        return pick(
            self.core, flip_bit(index, step), flip_bit(index, self.bits - 1 - step)
        )

    def subset(self, index, steps):
        for step in steps:
            index = self.flipped(index, step)
        return index


def subsets(steps):
    found = [()]
    for step in steps:
        found = found + [more + (step,) for more in found]
    return found


def remote(src, dst, send, recv, device):
    return pltpu.make_async_remote_copy(
        src_ref=src, dst_ref=dst, send_sem=send, recv_sem=recv,
        device_id=device, device_id_type=MESH,
    )


def greet(devices, conditions):
    barrier = pltpu.get_barrier_semaphore()
    count = 0
    for device, condition in zip(devices, conditions):
        if condition is None:
            pl.semaphore_signal(barrier, inc=1, device_id=device, device_id_type=MESH)
            count = count + 1
        else:
            @pl.when(condition)
            def _(device=device):
                pl.semaphore_signal(barrier, inc=1, device_id=device, device_id_type=MESH)
            count = count + jnp.where(condition, 1, 0)
    pl.semaphore_wait(barrier, count)


def cond(condition, action):
    @pl.when(condition)
    def _():
        action()


def nn(a, b):
    return lax.dot_general(a, b, (((1,), (0,)), ((), ())), preferred_element_type=F32)


def nt(a, b):
    return lax.dot_general(a, b, (((1,), (1,)), ((), ())), preferred_element_type=F32)


def normalise(values):
    centered = values - jnp.mean(values, axis=-1, keepdims=True)
    scale = lax.rsqrt(jnp.mean(centered * centered, axis=-1, keepdims=True) + EPS)
    return centered * scale, scale


def norm_back(hat, scale, gain, grad):
    scaled = grad * gain
    mean = jnp.mean(scaled, axis=-1, keepdims=True)
    along = jnp.mean(scaled * hat, axis=-1, keepdims=True)
    return (scaled - mean - hat * along) * scale


def column_sums(values):
    return jnp.sum(values, axis=0, keepdims=True)


def pair_rows(values, pair):
    both = values[:, pair * 128 : pair * 128 + 128]
    first = lax.broadcasted_iota(jnp.int32, both.shape, 1) < 64
    zero = jnp.zeros_like(both)
    return jnp.concatenate([jnp.where(first, both, zero), jnp.where(first, zero, both)], axis=0)


def unpair(turned):
    both = jnp.transpose(turned)
    rows = both.shape[0] // 2
    first = lax.broadcasted_iota(jnp.int32, (rows, 128), 1) < 64
    return jnp.where(first, both[:rows], both[rows:])


def earlier(block, rows):
    key = lax.broadcasted_iota(jnp.int32, (block, 2 * rows), 0)
    query = lax.broadcasted_iota(jnp.int32, (block, 2 * rows), 1)
    return key <= jnp.where(query >= rows, query - rows, query)


def attend_start(top, total, acc):
    top[...] = jnp.full(top.shape, NEGATIVE, F32)
    total[...] = jnp.zeros(total.shape, F32)
    acc[...] = jnp.zeros(acc.shape, F32)


def attend_block(queries, keys, turned_values, hot, top, total, acc, diagonal):
    for pair in range(queries.shape[0]):
        lanes = slice(pair * 128, pair * 128 + 128)
        left = keys[:, lanes]
        if hot is not None:
            left = jnp.concatenate([left, hot], axis=1)
        scores = nt(left, queries[pair])
        if diagonal:
            scores = jnp.where(earlier(left.shape[0], scores.shape[1] // 2), scores, NEGATIVE)
        before = top[pair : pair + 1, :]
        after = jnp.maximum(before, jnp.max(scores, axis=0, keepdims=True))
        factor = jnp.exp(before - after)
        weights = jnp.exp(scores - after)
        top[pair : pair + 1, :] = after
        total[pair : pair + 1, :] = total[pair : pair + 1, :] * factor + jnp.sum(weights, axis=0, keepdims=True)
        acc[pair] = acc[pair] * factor + nn(turned_values[lanes, :], weights.astype(BF))


def attend_finish(top, total, acc, lse, out):
    for pair in range(acc.shape[0]):
        sums = total[pair : pair + 1, :]
        lse[pair : pair + 1, :] = top[pair : pair + 1, :] + jnp.log(sums)
        out[:, pair * 128 : pair * 128 + 128] = unpair(acc[pair] / sums)


def attend_back_block(queries, grads, keys, values, turned_keys, hot, lse, delta, grad_q, grad_k, grad_v, diagonal):
    for pair in range(queries.shape[0]):
        lanes = slice(pair * 128, pair * 128 + 128)
        left = keys[:, lanes]
        if hot is not None:
            left = jnp.concatenate([left, hot], axis=1)
        scores = nt(left, queries[pair])
        if diagonal:
            scores = jnp.where(earlier(left.shape[0], scores.shape[1] // 2), scores, NEGATIVE)
        probs = jnp.exp(scores - lse[pair : pair + 1, :])
        grad_probs = nt(values[:, lanes], grads[pair])
        grad_scores = (probs * (grad_probs - delta[pair : pair + 1, :])).astype(BF)
        grad_v[:, lanes] = nn(probs.astype(BF), grads[pair]).astype(BF)
        grad_k[:, lanes] = nn(grad_scores, queries[pair, :, 0:128]).astype(BF)
        grad_q[pair] += nn(turned_keys[lanes, :], grad_scores)


def deltas(grad, out, delta, pairs):
    turned = jnp.transpose(grad.astype(F32) * out)
    for pair in range(pairs):
        at = pair * 128
        one = jnp.sum(turned[at : at + 64], axis=0, keepdims=True)
        two = jnp.sum(turned[at + 64 : at + 128], axis=0, keepdims=True)
        delta[pair : pair + 1, :] = jnp.concatenate([one, two], axis=1)


def store_owners(grads, group, unit, matrix, shards):
    rows = matrix.shape[0] // shards
    for s in range(shards):
        grads[group, s // 2, s % 2, unit * rows : (unit + 1) * rows, :] = matrix[s * rows : (s + 1) * rows].astype(BF)


def erf_parts(pre):
    cdf = 0.5 * (1.0 + lax.erf(pre * (0.5**0.5)))
    slope = cdf + pre * jnp.exp(-0.5 * pre * pre) * (1.0 / math.sqrt(2.0 * math.pi))
    return cdf, slope


G_OUT, G_IN, G_CROSS, G_SELF = range(4)
V_PROJ, V_OUT, V_GAIN, V_SHIFT, V_IN = 0, 4, 7, 10, 13


def shape_of(kind, *shape):
    return jax.ShapeDtypeStruct(shape, kind)


SELF, CROSS, FC_IN, FC_OUT, HIDDEN, ENCODED, SMALL = range(7)
WEIGHTS = (SELF, CROSS, FC_IN, FC_OUT)


def forward_kernel(
    shards, reps, *refs,
):
    qkv_out = {0: refs[0:2], 1: refs[2:4]}
    ins = (refs[0], refs[2], *refs[4:9])
    segs, parents, cotangent = refs[9:12]
    (result, grad_across, grads, keys, values, queries, hot, lse, att, c_queries, c_keys, c_values, c_lse, catt,
     after_self, normed1, sums, params, keep_self, keep_cross, keep_hidden, keep_states) = refs[12:34]
    (w_self, w_cross, w_in, w_out, hidden, states, small_all, bias_in,
     kbuf, vbuf, turned, c_turned, top, total, acc, grad_n2, held, gbuf_in, gbuf_out,
     k_sem, v_sem, g_sem, keep_sem, own_sem, mate_send, mate_recv, line_send, line_recv, rep_send, rep_recv,
     far_send, far_recv, small_send, small_recv) = refs[34:]
    outs = (w_self, w_cross, w_in, w_out, hidden, states, small_all)
    here = Place(shards, reps)
    line, bits = here.line, here.bits
    pos, core, rep, shard = here.pos, here.core, here.rep, here.shard
    rows, width = cotangent.shape
    frames = states.shape[0]
    strip = width * UNITS // reps
    w_rows = ins[SELF].shape[1]


    def block(refs_, item, s):
        ref = refs_[item]
        if item in (SELF, CROSS):
            return ref.at[:, pl.ds(pl.multiple_of(s * w_rows, 16), w_rows), :]
        n = ins[item].shape[0]
        return ref.at[pl.ds(pl.multiple_of(s * n, 16), n), :]

    def piece(refs_, item, r, s):
        if item == ENCODED:
            return block(refs_, item, s)
        ref = refs_[item]
        unit = r % UNITS
        at = 0 if reps == UNITS else pl.multiple_of((r // UNITS) * strip, 128)
        columns = pl.ds(at, strip)
        if item in (SELF, CROSS):
            return ref.at[unit, pl.ds(pl.multiple_of(s * w_rows, 16), w_rows), columns]
        if item == FC_IN:
            return ref.at[
                pl.ds(pl.multiple_of(s * w_rows, 16), w_rows), pl.ds(pl.multiple_of(unit * width + at, 128), strip)
            ]
        return ref.at[pl.ds(pl.multiple_of(s * UNITS * w_rows + unit * w_rows, 16), w_rows), columns]

    mate = here.partner()
    greet(
        [(rep, (shard + d) % shards) for d in range(1, shards)]
        + [(flip_bit(rep, bit), shard) for bit in range(bits)],
        [None] * (shards - 1 + bits),
    )

    def own_parts(item):
        qkv, last_one = qkv_out[item]
        at = pl.ds(pl.multiple_of(shard * w_rows, 16), w_rows)
        return [
            pltpu.make_async_copy(qkv, outs[item].at[pl.ds(0, UNITS - 1), at, :], own_sem.at[item]),
            pltpu.make_async_copy(last_one, outs[item].at[UNITS - 1, at, :], own_sem.at[7 + item]),
        ]

    own = {i: pltpu.make_async_copy(ins[i], block(outs, i, shard), own_sem.at[i]) for i in range(2, 6)}
    own[SMALL] = pltpu.make_async_copy(ins[SMALL], small_all.at[shard], own_sem.at[SMALL])
    to_mate = [
        remote(
            block(outs, i, shard) if i in qkv_out else ins[i], block(outs, i, shard), mate_send.at[i], mate_recv.at[i], mate
        )
        for i in range(6)
    ]
    small_out = [
        remote(ins[SMALL], small_all.at[shard], small_send.at[d], small_recv.at[d], (rep, (shard + d) % shards))
        for d in range(1, shards)
    ]

    def small_wait(d):
        s = (shard - d + shards) % shards
        remote(small_all.at[s], small_all.at[s], small_send.at[d], small_recv.at[d], mate).wait_recv()

    WAYS = (0, 1)

    def source(way, t):
        return (pos - t if way == 0 else pos + t) * 2 + core

    def arrives(way, t):
        return pos - t >= 0 if way == 0 else pos + t < line

    def onward(way):
        return pos + 1 < line if way == 0 else pos > 0

    def line_copy(item, way, t):
        region = piece(outs, item, rep, source(way, t))
        at = (item, way * line + t)
        return remote(
            piece(ins, item, rep, 0) if t == 0 and item not in qkv_out else region, region, line_send.at[at], line_recv.at[at],
            here.along(pos + 1 if way == 0 else pos - 1),
        )

    def take(item, way, t):
        region = piece(outs, item, rep, source(way, t))
        at = (item, way * line + t - 1)
        remote(region, region, line_send.at[at], line_recv.at[at], mate).wait_recv()
        if t + 1 < line:
            cond(onward(way), lambda: line_copy(item, way, t).start())

    def each_source(action):
        for t in range(1, line):
            for way in WAYS:
                cond(arrives(way, t), functools.partial(action, way, t))

    def hop(t):
        s = (pos - t) * 2 + core
        src = ins[HIDDEN] if t == 0 else block(outs, HIDDEN, s)
        return remote(
            src, block(outs, HIDDEN, s), line_send.at[HIDDEN, t], line_recv.at[HIDDEN, t], here.along(pos + 1)
        )

    def hop_wait(t):
        region = block(outs, HIDDEN, (pos - t) * 2 + core)
        remote(region, region, line_send.at[HIDDEN, t - 1], line_recv.at[HIDDEN, t - 1], mate).wait_recv()

    def far(item, at, s):
        return remote(block(outs, item, s), block(outs, item, s), far_send.at[item, at], far_recv.at[item, at], mate)

    def mate_block(s):
        return s + 1 - 2 * core

    def relay(t):
        def arrived():
            hop_wait(t)
            if t + 1 < line:
                cond(pos + 1 < line, lambda: hop(t).start())
            far(HIDDEN, t, (pos - t) * 2 + core).start()

        cond(pos - t >= 0, arrived)

    def relay_wait(t):
        far(HIDDEN, t, (pos - t) * 2 + 1 - core).wait_recv()

    def rep_at(step, more):
        return (1 << step) - 1 + subsets(range(step)).index(more)

    def rep_copy(item, way, t, step, more):
        region = piece(outs, item, here.subset(rep, more), source(way, t))
        at = (item, way * line + t, rep_at(step, more))
        return remote(region, region, rep_send.at[at], rep_recv.at[at], (here.flipped(rep, step), shard))

    def rep_wait(item, way, t, step, more):
        region = piece(outs, item, here.subset(here.flipped(rep, step), more), source(way, t))
        at = (item, way * line + t, rep_at(step, more))
        remote(region, region, rep_send.at[at], rep_recv.at[at], mate).wait_recv()

    def spread(item, step):
        def one(way, t):
            if step == 0:
                take(item, way, t)
            else:
                for more in subsets(range(step - 1)):
                    rep_wait(item, way, t, step - 1, more)
            if step < bits:
                for more in subsets(range(step)):
                    rep_copy(item, way, t, step, more).start()
            else:
                far(item, way * line + t, source(way, t)).start()

        each_source(one)

    def pass_on(item):
        def one(way, t):
            take(item, way, t)
            far(item, way * line + t, source(way, t)).start()

        each_source(one)

    def complete(item):
        if item not in qkv_out:
            own[item].wait()
        to_mate[item].wait_recv()
        each_source(lambda way, t: far(item, way * line + t, mate_block(source(way, t))).wait_recv())


    for item in (SELF, CROSS):
        for copy in own_parts(item):
            copy.start()
    own[SMALL].start()
    for copy in small_out:
        copy.start()
    for copy in own_parts(SELF):
        copy.wait()

    def send(item):
        for way in WAYS:
            cond(onward(way), lambda: line_copy(item, way, 0).start())

    send(SELF)
    cond(pos + 1 < line, lambda: hop(0).start())
    for copy in own_parts(CROSS):
        copy.wait()
    for i in (SELF, HIDDEN, CROSS, FC_IN, FC_OUT, ENCODED):
        to_mate[i].start()
        if i not in qkv_out:
            own[i].start()
    for item in (CROSS, FC_IN, FC_OUT, ENCODED):
        send(item)


    pairs = width // 128
    scale = 64 ** (-0.5)
    own_rows = pl.ds(pl.multiple_of(shard * rows, rows), rows)

    def block_of(b):
        return pl.ds(pl.multiple_of(b * rows, rows), rows)

    def gain(i):
        return params[11 + i : 12 + i, :]

    def shift(i):
        return params[14 + i : 15 + i, :]

    def write_k(b, slot):
        return pltpu.make_async_copy(kbuf.at[slot], keys.at[block_of(b)], k_sem.at[slot])

    def write_v(b, slot):
        return pltpu.make_async_copy(vbuf.at[slot], values.at[block_of(b)], v_sem.at[slot])

    count = segs.shape[1]
    ids = lax.broadcasted_iota(jnp.int32, (128, rows), 0)
    for b in range(count // rows):
        at = slice(b * rows, (b + 1) * rows)
        hot[at, :] = jnp.transpose((ids == segs[:, at]).astype(F32)).astype(BF)
    link = parents[...]
    line_ = lax.broadcasted_iota(jnp.int32, (128, 128), 0)
    across_ = lax.broadcasted_iota(jnp.int32, (128, 128), 1)
    reach = jnp.where(line_ == across_, 1.0, 0.0) + link.astype(F32) + nn(link, link)
    seen = nn(hot[own_rows, :], reach.astype(BF))
    hide = jnp.where(seen > 0.5, 0.0, NEGATIVE).astype(BF)
    hide = jnp.concatenate([hide, hide], axis=0)
    attend_start(top, total, acc)
    sums[...] = jnp.zeros_like(sums)
    grad_n2[...] = jnp.zeros_like(grad_n2)

    own[SMALL].wait()
    for d in range(1, shards):
        small_wait(d)
    part = width // shards
    for s in range(shards):
        some = small_all[s].astype(F32)
        params[:, s * part : (s + 1) * part] = some[:, :part]
        for u in range(UNITS):
            at = s * part * UNITS + u * part
            bias_in[:, at : at + part] = some[7 + u : 8 + u, :part]

    def norm0(values_):
        hat, _ = normalise(values_.astype(F32))
        return (hat * gain(0) + shift(0)).astype(BF)

    spread(SELF, 0)
    own[HIDDEN].wait()
    held[...] = norm0(hidden[own_rows, :])
    for step in range(1, bits):
        spread(SELF, step)
    relay(1)
    spread(CROSS, 0)
    spread(SELF, bits)
    to_mate[HIDDEN].wait_recv()
    complete(SELF)

    q = ((nn(held[...], w_self[0]) + params[0:1, :]).astype(BF) * scale).astype(BF)
    for pair in range(pairs):
        queries[pair, :, 0:128] = pair_rows(q, pair)
        queries[pair, :, 128:256] = hide

    def one_block(b, j, diagonal):
        slot = j % 2
        norm = held[...] if diagonal else norm0(hidden[block_of(b), :])

        @pl.when(j >= 2)
        def _():
            write_k(b, slot).wait()
            write_v(b, slot).wait()

        kbuf[slot] = nn(norm, w_self[1]).astype(BF)
        v = (nn(norm, w_self[2]) + params[1:2, :]).astype(BF)
        vbuf[slot] = v
        turned[...] = jnp.transpose(v)
        write_k(b, slot).start()
        write_v(b, slot).start()
        attend_block(queries, kbuf.at[slot], turned, hot[block_of(b), :], top, total, acc, diagonal)

    one_block(shard, jnp.int32(0), True)

    duties = {}

    def duty(j, action, *args):
        duties.setdefault(j, []).append(functools.partial(action, *args))

    last = shards - 1
    for t in range(2, line):
        duty(2 * t - 3, relay, t)
    duty(2, spread, CROSS, 1)
    duty(2, spread, FC_IN, 0)
    for step in range(2, bits + 1):
        duty(4, spread, CROSS, step)
    duty(4, spread, FC_IN, 1)
    duty(4, spread, FC_OUT, 0)
    duty(5, pass_on, ENCODED)
    for step in range(2, bits + 1):
        duty(6, spread, FC_IN, step)
    duty(7, spread, FC_OUT, 1)

    def step_block(j, carry):
        b = shard - j
        for when_, actions in sorted(duties.items()):
            @pl.when(j == when_)
            def _(actions=actions):
                for action in actions:
                    action()

        for t in range(1, line):
            @pl.when(jnp.logical_and(b >= 0, j == 2 * t - 1 + core))
            def _(t=t):
                relay_wait(t)

        @pl.when(b >= 0)
        def _():
            one_block(b, j, False)

        return carry

    lax.fori_loop(1, shards, step_block, 0)
    attend_finish(top, total, acc, lse, att)
    after_self[...] = hidden[own_rows, :].astype(F32) + nn(att[...].astype(BF), w_self[3]) + params[4:5, :]
    hat1, _ = normalise(after_self[...])
    normed1[...] = (hat1 * gain(1) + shift(1)).astype(BF)
    keep = [
        pltpu.make_async_copy(w_self, keep_self, keep_sem.at[0]),
        pltpu.make_async_copy(w_cross, keep_cross, keep_sem.at[1]),
        pltpu.make_async_copy(states, keep_states, keep_sem.at[2]),
        pltpu.make_async_copy(hidden.at[own_rows], keep_hidden.at[own_rows], keep_sem.at[3]),
    ]
    keep[0].start()
    keep[3].start()

    def keep_block(b):
        return pltpu.make_async_copy(hidden.at[block_of(b)], keep_hidden.at[block_of(b)], keep_sem.at[4 + b])

    for b in range(shards):
        cond(b < shard, lambda: keep_block(b).start())

    complete(CROSS)
    keep[1].start()
    cq = ((nn(normed1[...], w_cross[0]) + params[2:3, :]).astype(BF) * scale).astype(BF)
    for pair in range(pairs):
        c_queries[pair] = pair_rows(cq, pair)
    attend_start(top, total, acc)
    complete(ENCODED)
    keep[2].start()

    def c_block(b, carry):
        at = block_of(b)
        c_keys[at, :] = nn(states[at, :], w_cross[1]).astype(BF)
        v = (nn(states[at, :], w_cross[2]) + params[3:4, :]).astype(BF)
        c_values[at, :] = v
        c_turned[...] = jnp.transpose(v)
        attend_block(c_queries, c_keys.at[at], c_turned, None, top, total, acc, False)

        for step in range(2, bits + 1):
            @pl.when(b == min(step - 2, frames // rows - 1))
            def _(step=step):
                spread(FC_OUT, step)

        return carry

    lax.fori_loop(0, frames // rows, c_block, 0)
    attend_finish(top, total, acc, c_lse, catt)
    after_cross = after_self[...] + nn(catt[...].astype(BF), w_cross[3]) + params[5:6, :]
    hat2, scale2 = normalise(after_cross)
    normed2 = (hat2 * gain(2) + shift(2)).astype(BF)
    held[...] = normed2
    result[...] = after_cross + params[6:7, :]
    turned2 = jnp.transpose(normed2)
    each = gbuf_out.shape[1]
    complete(FC_IN)
    complete(FC_OUT)

    def send_grads(u):
        return (
            pltpu.make_async_copy(gbuf_out.at[u % 2], grads.at[0, pl.ds(u * each, each)], g_sem.at[0, u % 2]),
            pltpu.make_async_copy(gbuf_in.at[u % 2], grads.at[1, :, :, pl.ds(u * part, part)], g_sem.at[1, u % 2]),
        )

    for u in range(UNITS):
        at = slice(u * width, (u + 1) * width)
        norm2 = held[...]
        pre = nn(norm2, w_in[:, at]) + bias_in[:, at]
        cdf, slope = erf_parts(pre)
        act = (pre * cdf).astype(BF)
        result[...] += nn(act, w_out[at, :])
        grad_pre = (slope * nt(cotangent[...], w_out[at, :])).astype(BF)
        grad_n2[...] += nt(grad_pre, w_in[:, at])
        if u >= 2:
            for copy in send_grads(u - 2):
                copy.wait()
        g = nn(turned2, grad_pre)
        for s in range(shards):
            gbuf_in[u % 2, s // 2, s % 2] = g[s * part : (s + 1) * part].astype(BF)
        g = nn(jnp.transpose(act), cotangent[...])
        tall = part * UNITS
        for j in range(width // tall):
            gbuf_out[u % 2, j // 2, j % 2] = g[j * tall : (j + 1) * tall].astype(BF)
        for copy in send_grads(u):
            copy.start()
        sums[V_IN + u : V_IN + u + 1, :] = column_sums(grad_pre.astype(F32))

    grad = cotangent[...].astype(F32)
    dn = grad_n2[...]
    grad_across[...] = grad + norm_back(hat2, scale2, gain(2), dn)
    sums[V_OUT + 2 : V_OUT + 3, :] = column_sums(grad)
    sums[V_GAIN + 2 : V_GAIN + 3, :] = column_sums(dn * hat2)
    sums[V_SHIFT + 2 : V_SHIFT + 3, :] = column_sums(dn)

    for u in (UNITS - 2, UNITS - 1):
        for copy in send_grads(u):
            copy.wait()
    write_k(shard, shard % 2).wait()
    write_v(shard, shard % 2).wait()

    @pl.when(shard >= 1)
    def _():
        write_k(shard - 1, (shard + 1) % 2).wait()
        write_v(shard - 1, (shard + 1) % 2).wait()

    for copy in keep:
        copy.wait()
    for b in range(shards):
        cond(b < shard, lambda: keep_block(b).wait())
    for i in range(6):
        to_mate[i].wait_send()
    for copy in small_out:
        copy.wait_send()
    for item in WEIGHTS + (ENCODED,):
        for way in WAYS:
            cond(onward(way), lambda: line_copy(item, way, 0).wait_send())

        def drain(way, t):
            if t + 1 < line:
                cond(onward(way), lambda: line_copy(item, way, t).wait_send())
            far(item, way * line + t, source(way, t)).wait_send()
            if item in WEIGHTS:
                for step in range(bits):
                    for more in subsets(range(step)):
                        rep_copy(item, way, t, step, more).wait_send()

        each_source(drain)
    cond(pos + 1 < line, lambda: hop(0).wait_send())
    for t in range(1, line):
        def drain_tokens():
            if t + 1 < line:
                cond(pos + 1 < line, lambda: hop(t).wait_send())
            far(HIDDEN, t, (pos - t) * 2 + core).wait_send()

        cond(pos - t >= 0, drain_tokens)


def forward(mesh_shape, self_qkv, self_out, cross_qkv, cross_out, fc_in, fc_out, hidden, encoded, small, segs, parents, cotangent):
    shards, reps = mesh_shape
    line, bits = shards // 2, reps.bit_length() - 1
    rows, width = cotangent.shape
    count, frames = rows * shards, encoded.shape[0] * shards
    pairs = width // 128
    unit_rows = fc_out.shape[0]
    part = width // shards
    each = width // unit_rows // 2
    f32, bf = functools.partial(shape_of, F32), functools.partial(shape_of, BF)
    vm, hbm = pl.BlockSpec(memory_space=pltpu.VMEM), pl.BlockSpec(memory_space=pl.ANY)
    dma = pltpu.SemaphoreType.DMA

    def bv(*shape):
        return pltpu.VMEM(shape, BF)

    def fv(*shape):
        return pltpu.VMEM(shape, F32)

    return pl.pallas_call(
        functools.partial(forward_kernel, shards, reps),
        out_shape=(
            f32(rows, width), f32(rows, width), bf(2, line, 2, unit_rows, width), bf(count, width),
            bf(count, width), bf(pairs, 2 * rows, 256), bf(count, 128), f32(8, 2 * rows), f32(rows, width),
            bf(pairs, 2 * rows, 128), bf(frames, width), bf(frames, width), f32(8, 2 * rows),
            f32(rows, width), f32(rows, width), bf(rows, width), f32(GRAD_ROWS, width), f32(SMALL_ROWS, width),
            bf(UNITS, width, width), bf(UNITS, width, width), bf(count, width), bf(frames, width),
        ),
        in_specs=[hbm] * 9 + [vm] * 3,
        out_specs=[vm, vm, hbm, hbm, hbm] + [vm] * 13 + [hbm] * 4,
        scratch_shapes=[
            bv(UNITS, width, width), bv(UNITS, width, width), bv(width, UNITS * width), bv(UNITS * width, width),
            bv(count, width), bv(frames, width), bv(shards, SMALL_ROWS, 128), fv(1, UNITS * width),
            bv(2, rows, width), bv(2, rows, width), bv(width, rows), bv(width, rows),
            fv(8, 2 * rows), fv(8, 2 * rows), fv(pairs, 128, 2 * rows), fv(rows, width), bv(rows, width),
            bv(2, line, 2, part, width), bv(2, each, 2, unit_rows, width),
            dma((2,)), dma((2,)), dma((2, 2)), dma((4 + shards,)), dma((9,)), dma((7,)), dma((7,)),
            dma((6, 2 * line)), dma((6, 2 * line)), dma((4, 2 * line, reps)), dma((4, 2 * line, reps)),
            dma((6, 2 * line)), dma((6, 2 * line)), dma((shards,)), dma((shards,)),
        ],
        compiler_params=pltpu.CompilerParams(
            collective_id=0, has_side_effects=True, vmem_limit_bytes=60 * 2**20
        ),
        name="forward",
    )(self_qkv, self_out, cross_qkv, cross_out, fc_in, fc_out, hidden, encoded, small, segs, parents, cotangent)


def backward_kernel(shards, reps, *refs):
    (ffn, hidden, states, keys, values, c_keys, c_values, keep_self, keep_cross) = refs[:9]
    (params, grad_across, queries, hot, lse, att, c_queries, c_lse, catt, after_self, normed1, sums_in) = refs[9:21]
    (d_hidden, out_denc, out_small, out, got_mate, got_rep, x_mate, x_line) = refs[21:29]
    (weights, mine, accf, stage, got_line, shared, finish, x_own, x_send, d_states, e_mate, e_own, e_line,
     s_src, s_line, s_rep, sums, dn_own, grad_after_self,
     hbuf, kbuf, vbuf, turned, pair_grads, delta, grad_q, grad_k, grad_v, gk_acc, gv_acc,
     r_sem, w_sem, load_sem, stage_sem, out_sem, mate_send, mate_recv, rep_send, rep_recv, line_send, line_recv,
     share_send, share_recv, xm_send, xm_recv, xl_send, xl_recv, em_send, em_recv, el_send, el_recv,
     s_send, s_recv, t_send, t_recv) = refs[29:]
    here = Place(shards, reps)
    line, bits = here.line, here.bits
    pos, core, rep, shard = here.pos, here.core, here.rep, here.shard
    rows, width = grad_across.shape
    frames = states.shape[0]
    fr = frames // shards
    part = width // shards
    strip = width * UNITS // reps
    scale = 64 ** (-0.5)
    pairs = width // 128
    other = 1 - core
    mate = here.partner()

    halves = 2 if reps == UNITS and width % 256 == 0 else 1
    jobs = [(G_OUT, 0, strip), (G_IN, 0, strip), (G_CROSS, 0, strip)]
    jobs += [(G_SELF, h * (strip // halves), strip // halves) for h in range(halves)]

    greet(
        [(rep, (shard + d) % shards) for d in range(1, shards)]
        + [((rep + e) % reps, shard) for e in range(1, reps)],
        [None] * (shards + reps - 2),
    )

    def held(g):
        return accf.at[g] if g < 2 else mine.at[g - 2, :, core]

    def leaving(g):
        return ffn.at[g, :, other] if g < 2 else mine.at[g - 2, :, other]

    def span(job):
        g, at, size = jobs[job]
        return pl.ds(0, width) if reps != UNITS else pl.ds(at, size)

    def swap(job):
        g = jobs[job][0]
        return remote(
            leaving(g).at[:, :, span(job)], got_mate.at[g, :, :, span(job)], mate_send.at[job], mate_recv.at[job], mate
        )

    def columns(r, job):
        g, at, size = jobs[job]
        if reps == UNITS:
            return pl.ds(at, size)
        return pl.ds(pl.multiple_of((r // UNITS) * strip + at, 128), size)

    def piece(job, r):
        return held(jobs[job][0]).at[:, pl.ds(pl.multiple_of((r % UNITS) * part, 16), part), columns(r, job)]

    def plus(a, b):
        return (a.astype(F32) + b.astype(F32)).astype(BF)

    def add_all(into, other_ref):
        def add(i, carry):
            into[i] = plus(into[i], other_ref[i])
            return carry

        lax.fori_loop(0, line, add, 0)

    load = [pltpu.make_async_copy(ffn.at[g, :, core], accf.at[g], load_sem.at[g]) for g in range(2)]

    def rep_copy(job, step, more):
        g, at, size = jobs[job]
        slot = (1 << bits) - (1 << (bits - step)) + subsets(range(step + 1, bits)).index(more)
        target = here.flipped(rep, step)
        return remote(
            piece(job, here.subset(target, more)), got_rep.at[g, slot, :, :, pl.ds(at, size)],
            rep_send.at[job, slot], rep_recv.at[job, slot], (target, shard),
        ), slot

    def send_rep(job, step):
        for more in subsets(range(step + 1, bits)):
            rep_copy(job, step, more)[0].start()

    def line_copy(job, d):
        g, at, size = jobs[job]
        to = (pos + d) % line
        return remote(
            piece(job, rep).at[to], got_line.at[g, d, :, pl.ds(at, size)], line_send.at[job, d], line_recv.at[job, d],
            here.along(to),
        )

    def share_copy(job, e):
        g, at, size = jobs[job]
        own = shared.at[g, rep, :, pl.ds(at, size)]
        return remote(own, own, share_send.at[job, e], share_recv.at[job, e], ((rep + e) % reps, shard))

    def share_wait(job, e):
        g, at, size = jobs[job]
        got = shared.at[g, (rep - e + reps) % reps, :, pl.ds(at, size)]
        remote(got, got, share_send.at[job, e], share_recv.at[job, e], ((rep + e) % reps, shard)).wait_recv()

    def stage_mate(job):
        g = jobs[job][0]
        if g < 2:
            load[g].wait()
        swap(job).wait()
        staged = stage.at[:, :, span(job)]
        copy = pltpu.make_async_copy(got_mate.at[g, :, :, span(job)], staged, stage_sem.at[0])
        copy.start()
        copy.wait()
        add_all(held(g).at[:, :, span(job)], staged)
        send_rep(job, 0)

    def stage_rep(job, step):
        g, at, size = jobs[job]
        staged = []
        for i, more in enumerate(subsets(range(step + 1, bits))):
            copy, slot = rep_copy(job, step, more)
            copy.wait()
            into = stage.at[:, pl.ds((i % UNITS) * part, part), pl.ds((i // UNITS) * size, size)]
            staged.append((more, into, pltpu.make_async_copy(
                got_rep.at[g, slot, :, :, pl.ds(at, size)], into, stage_sem.at[i]
            )))
            staged[-1][2].start()
        for more, into, copy in staged:
            copy.wait()
            add_all(piece(job, here.subset(rep, more)), into)
        if step + 1 < bits:
            send_rep(job, step + 1)
        else:
            for d in range(1, line):
                line_copy(job, d).start()

    def stage_line(job):
        g, at, size = jobs[job]
        total = piece(job, rep)[pos].astype(F32)
        for d in range(1, line):
            line_copy(job, d).wait()
            total = total + got_line[g, d, :, at : at + size].astype(F32)
        shared[g, rep, :, at : at + size] = total.astype(BF)
        for e in range(1, reps):
            share_copy(job, e).start()

    def out_copy(job):
        g = jobs[job][0]
        return pltpu.make_async_copy(finish.at[job % 2, :, span(job)], out.at[g, :, span(job)], out_sem.at[job])

    def stage_share(job):
        g, at, size = jobs[job]
        for e in range(1, reps):
            share_copy(job, e).wait_send()
            share_wait(job, e)
        if job >= 2:
            out_copy(job - 2).wait()
        for r in range(reps):
            unit, first = r % UNITS, (r // UNITS) * strip + at
            finish[job % 2, unit * part : (unit + 1) * part, first : first + size] = (
                shared[g, r, :, at : at + size].astype(F32)
            )
        out_copy(job).start()


    def x_swap(at):
        return remote(x_send.at[at], x_mate.at[at], xm_send.at[at], xm_recv.at[at], mate)

    def x_down(t):
        return remote(x_own.at[pos - t], x_line.at[t - 1], xl_send.at[t], xl_recv.at[t - 1], here.along(pos - 1))

    def x_flush(t):
        def flush():
            at = pos - t
            x_swap(at).wait()
            copy = pltpu.make_async_copy(x_mate.at[at], hbuf.at[2], stage_sem.at[0])
            copy.start()
            copy.wait()
            x_own[at] = plus(x_own[at], hbuf[2])

        cond(pos - t >= 0, flush)

    def x_chain(t):
        def link_():
            def take():
                remote(x_line.at[t], x_line.at[t], xl_send.at[t], xl_recv.at[t], mate).wait_recv()
                copy = pltpu.make_async_copy(x_line.at[t], hbuf.at[2], stage_sem.at[0])
                copy.start()
                copy.wait()
                x_own[pos - t] = plus(x_own[pos - t], hbuf[2])

            if t + 1 < line:
                cond(pos + 1 < line, take)
            if t > 0:
                x_down(t).start()

        cond(pos - t >= 0, link_)

    top_end = pos == line - 1


    def e_swap(i):
        return remote(
            d_states.at[pl.ds(pl.multiple_of((2 * i + other) * fr, 16), fr)], e_mate.at[i], em_send.at[i], em_recv.at[i],
            mate,
        )

    def e_out(d):
        to = (pos + d) % line
        return remote(e_own.at[to], e_line.at[d], el_send.at[d], el_recv.at[d], here.along(to))

    def e_stage():
        for i in range(line):
            e_swap(i).wait()
            mine_rows = d_states[pl.ds(pl.multiple_of((2 * i + core) * fr, 16), fr), :]
            e_own[i] = plus(mine_rows, e_mate[i])
        for d in range(1, line):
            e_out(d).start()

    def e_finish():
        total = e_own[pos].astype(F32)
        for d in range(1, line):
            e_out(d).wait()
            total = total + e_line[d].astype(F32)
        out_denc[...] = total


    def s_out(d):
        to = (shard + d) % shards
        return remote(s_src.at[to], s_line.at[d], s_send.at[d], s_recv.at[d], (rep, to))

    def s_share(e):
        return remote(s_rep.at[rep], s_rep.at[rep], t_send.at[e], t_recv.at[e], ((rep + e) % reps, shard))

    def s_start():
        for s in range(shards):
            s_src[s, 0:13, 0:part] = sums[0:13, s * part : (s + 1) * part]
            for u in range(UNITS):
                at = (s * UNITS + u) * part
                row = V_IN + at // width
                s_src[s, V_IN + u : V_IN + u + 1, 0:part] = sums[row : row + 1, at % width : at % width + part]
        for d in range(1, shards):
            s_out(d).start()

    def s_middle():
        total = s_src[shard]
        for d in range(1, shards):
            s_out(d).wait()
            total = total + s_line[d]
        s_rep[rep] = total
        for e in range(1, reps):
            s_share(e).start()

    def s_finish():
        for e in range(1, reps):
            s_share(e).wait_send()
            got = s_rep.at[(rep - e + reps) % reps]
            remote(got, got, t_send.at[e], t_recv.at[e], ((rep + e) % reps, shard)).wait_recv()
        total = s_rep[0]
        for r in range(1, reps):
            total = total + s_rep[r]
        out_small[...] = total


    for g in range(2):
        swap(g).start()
        load[g].start()

    def block_of(b):
        return pl.ds(pl.multiple_of(b * rows, rows), rows)

    def reads(cross, b, slot):
        sources = (states, c_keys, c_values) if cross else (hidden, keys, values)
        return [
            pltpu.make_async_copy(src.at[block_of(b)], buf.at[slot], r_sem.at[i, slot])
            for i, (src, buf) in enumerate(zip(sources, (hbuf, kbuf, vbuf)))
        ]

    def weight(source, unit):
        return pltpu.make_async_copy(source.at[unit], weights.at[unit], w_sem.at[unit])

    for unit in (3, 1, 2, 0):
        weight(keep_cross, unit).start()
    for copy in reads(True, 0, 0):
        copy.start()

    def gain(i):
        return params[11 + i : 12 + i, :]

    s_src[...] = jnp.zeros_like(s_src)
    sums[...] = sums_in[...]
    grad = grad_across[...]
    branch = grad.astype(BF)
    sums[V_OUT + 1 : V_OUT + 2, :] = column_sums(branch.astype(F32))
    store_owners(mine, 0, 3, nn(jnp.transpose(catt[...].astype(BF)), branch), shards)
    weight(keep_cross, 3).wait()
    g_catt = nt(branch, weights[3]).astype(BF)
    weight(keep_self, 3).start()
    deltas(g_catt, catt[...], delta, pairs)
    for pair in range(pairs):
        pair_grads[pair] = pair_rows(g_catt, pair)
    grad_q[...] = jnp.zeros_like(grad_q)
    gk_acc[...] = jnp.zeros_like(gk_acc)
    gv_acc[...] = jnp.zeros_like(gv_acc)
    sums[V_PROJ + 3 : V_PROJ + 4, :] = jnp.zeros((1, width), F32)
    stage_mate(0)
    weight(keep_cross, 1).wait()
    weight(keep_cross, 2).wait()
    c_blocks = frames // rows

    def c_block(b, carry):
        slot = b % 2
        for copy in reads(True, b, slot):
            copy.wait()

        @pl.when(b + 1 < c_blocks)
        def _():
            for copy in reads(True, b + 1, 1 - slot):
                copy.start()

        turned[...] = jnp.transpose(kbuf[slot])
        attend_back_block(
            c_queries, pair_grads, kbuf.at[slot], vbuf.at[slot], turned, None, c_lse, delta, grad_q, grad_k, grad_v, False
        )
        gk, gv = grad_k[...], grad_v[...]
        flipped = jnp.transpose(hbuf[slot])
        gk_acc[...] += nn(flipped, gk)
        gv_acc[...] += nn(flipped, gv)
        d_states[block_of(b), :] = (nt(gk, weights[1]) + nt(gv, weights[2])).astype(BF)
        sums[V_PROJ + 3 : V_PROJ + 4, :] += column_sums(gv.astype(F32))

        @pl.when(b == 0)
        def _():
            stage_mate(1)

        return carry

    lax.fori_loop(0, c_blocks, c_block, 0)
    for unit in (1, 2):
        weight(keep_self, unit).start()
    for copy in reads(False, shard, 0):
        copy.start()
    for i in range(line):
        e_swap(i).start()
    store_owners(mine, 0, 1, gk_acc[...], shards)
    store_owners(mine, 0, 2, gv_acc[...], shards)
    gcq = jnp.concatenate([(unpair(grad_q[pair]) * scale).astype(BF) for pair in range(pairs)], axis=1)
    sums[V_PROJ + 2 : V_PROJ + 3, :] = column_sums(gcq.astype(F32))
    store_owners(mine, 0, 0, nn(jnp.transpose(normed1[...]), gcq), shards)
    swap(2).start()
    weight(keep_cross, 0).wait()
    dn1 = nt(gcq, weights[0])
    weight(keep_self, 0).start()
    hat1, scale1 = normalise(after_self[...])
    sums[V_GAIN + 1 : V_GAIN + 2, :] = column_sums(dn1 * hat1)
    sums[V_SHIFT + 1 : V_SHIFT + 2, :] = column_sums(dn1)
    grad_after_self[...] = grad + norm_back(hat1, scale1, gain(1), dn1)
    stage_rep(0, 0)

    self_branch = grad_after_self[...].astype(BF)
    sums[V_OUT : V_OUT + 1, :] = column_sums(self_branch.astype(F32))
    store_owners(mine, 1, 3, nn(jnp.transpose(att[...].astype(BF)), self_branch), shards)
    weight(keep_self, 3).wait()
    g_att = nt(self_branch, weights[3]).astype(BF)
    deltas(g_att, att[...], delta, pairs)
    for pair in range(pairs):
        pair_grads[pair] = pair_rows(g_att, pair)
    grad_q[...] = jnp.zeros_like(grad_q)
    gk_acc[...] = jnp.zeros_like(gk_acc)
    gv_acc[...] = jnp.zeros_like(gv_acc)
    sums[V_PROJ + 1 : V_PROJ + 2, :] = jnp.zeros((1, width), F32)
    sums[V_GAIN : V_GAIN + 1, :] = jnp.zeros((1, width), F32)
    sums[V_SHIFT : V_SHIFT + 1, :] = jnp.zeros((1, width), F32)
    weight(keep_self, 1).wait()
    weight(keep_self, 2).wait()

    def one_block(b, j, diagonal):
        slot = j % 2
        for copy in reads(False, b, slot):
            copy.wait()

        @pl.when(b >= 1)
        def _():
            for copy in reads(False, b - 1, 1 - slot):
                copy.start()

        turned[...] = jnp.transpose(kbuf[slot])
        attend_back_block(
            queries, pair_grads, kbuf.at[slot], vbuf.at[slot], turned, hot[block_of(b), :], lse, delta,
            grad_q, grad_k, grad_v, diagonal,
        )
        hat, _ = normalise(hbuf[slot].astype(F32))
        norm = (hat * gain(0) + params[14:15, :]).astype(BF)
        gk, gv = grad_k[...], grad_v[...]
        flipped = jnp.transpose(norm)
        gk_acc[...] += nn(flipped, gk)
        gv_acc[...] += nn(flipped, gv)
        dn = nt(gk, weights[1]) + nt(gv, weights[2])

        @pl.when(b % 2 == core)
        def _():
            x_own[b // 2] = dn.astype(BF)

        @pl.when(b % 2 != core)
        def _():
            x_send[b // 2] = dn.astype(BF)
            x_swap(b // 2).start()

        sums[V_PROJ + 1 : V_PROJ + 2, :] += column_sums(gv.astype(F32))
        sums[V_GAIN : V_GAIN + 1, :] += column_sums(dn * hat)
        sums[V_SHIFT : V_SHIFT + 1, :] += column_sums(dn)

    one_block(shard, jnp.int32(0), True)

    @pl.when(core == 0)
    def _():
        x_send[pos] = jnp.zeros((rows, width), BF)
        x_swap(pos).start()

    stage_mate(2)
    duties = {}

    def duty(j, action, *args):
        duties.setdefault(max(1, min(j, shards - 1)), []).append(functools.partial(action, *args))

    last = shards - 1
    duty(2, stage_rep, 1, 0)
    for t in range(0, line - 1):
        duty(2 * t + 2, x_flush, t)
        if t > 0:
            duty(2 * t + 2, cond, top_end, functools.partial(x_chain, t))
    duty(3, e_stage)
    for step in range(1, bits):
        duty(1 + 2 * step, stage_rep, 0, step)
        duty(4 + 2 * step, stage_rep, 1, step)

    def step_block(j, carry):
        b = shard - j
        for when_, actions in sorted(duties.items()):
            @pl.when(j == when_)
            def _(actions=actions):
                for action in actions:
                    action()

        @pl.when(b >= 0)
        def _():
            one_block(b, j, False)

        return carry

    lax.fori_loop(1, shards, step_block, 0)
    store_owners(mine, 1, 1, gk_acc[...], shards)
    store_owners(mine, 1, 2, gv_acc[...], shards)
    gq = jnp.concatenate([(unpair(grad_q[pair]) * scale).astype(BF) for pair in range(pairs)], axis=1)
    sums[V_PROJ : V_PROJ + 1, :] = column_sums(gq.astype(F32))
    own_hidden = pltpu.make_async_copy(hidden.at[block_of(shard)], hbuf.at[0], r_sem.at[0, 0])
    own_hidden.start()
    own_hidden.wait()
    hat0, scale0 = normalise(hbuf[0].astype(F32))
    norm = (hat0 * gain(0) + params[14:15, :]).astype(BF)
    store_owners(mine, 1, 0, nn(jnp.transpose(norm), gq), shards)
    first_self = 3
    for job in range(first_self, len(jobs)):
        swap(job).start()
    weight(keep_self, 0).wait()
    dn = nt(gq, weights[0])
    dn_own[...] = dn
    sums[V_GAIN : V_GAIN + 1, :] += column_sums(dn * hat0)
    sums[V_SHIFT : V_SHIFT + 1, :] += column_sums(dn)
    s_start()
    selves = range(first_self, len(jobs))
    stage_rep(2, 0)
    for job in selves:
        stage_mate(job)
    x_flush(line - 1)
    cond(top_end, lambda: x_chain(line - 1))
    stage_line(0)
    stage_line(1)
    for step in range(1, bits):
        stage_rep(2, step)
    s_middle()
    for step in range(bits):
        for job in selves:
            stage_rep(job, step)
            if step == 0 and job == len(jobs) - 1:
                for t in range(1, line - 1):
                    cond(pos < line - 1, lambda: x_chain(t))
    stage_line(2)
    for job in selves:
        stage_line(job)
    stage_share(0)
    stage_share(1)
    s_finish()
    e_finish()
    x_chain(0)

    for t in range(1, line):
        cond(pos - t >= 0, lambda: x_down(t).wait_send())
    d_hidden[...] = dn_own[...] + x_own[pos].astype(F32)
    d_hidden[...] = grad_after_self[...] + norm_back(hat0, scale0, gain(0), d_hidden[...])
    stage_share(2)
    for job in selves:
        stage_share(job)
    for job in range(len(jobs) - 2, len(jobs)):
        out_copy(job).wait()


def backward(mesh_shape, ffn, hidden, states, keys, values, c_keys, c_values, keep_self, keep_cross, *saved):
    shards, reps = mesh_shape
    line, bits = shards // 2, reps.bit_length() - 1
    rows, width = saved[1].shape
    frames = states.shape[0]
    fr = frames // shards
    pairs = width // 128
    part = width // shards
    unit_rows = UNITS * part
    strip = width * UNITS // reps
    f32, bf = functools.partial(shape_of, F32), functools.partial(shape_of, BF)
    vm, hbm = pl.BlockSpec(memory_space=pltpu.VMEM), pl.BlockSpec(memory_space=pl.ANY)
    dma = pltpu.SemaphoreType.DMA
    most = 5

    def bv(*shape):
        return pltpu.VMEM(shape, BF)

    def fv(*shape):
        return pltpu.VMEM(shape, F32)

    return pl.pallas_call(
        functools.partial(backward_kernel, shards, reps),
        out_shape=(
            f32(rows, width), f32(fr, width), f32(GRAD_ROWS, 128), f32(4, unit_rows, width),
            bf(4, line, unit_rows, width), bf(4, reps, line, part, strip), bf(line, rows, width), bf(line, rows, width),
        ),
        in_specs=[hbm] * 9 + [vm] * 12,
        out_specs=[vm, vm, vm] + [hbm] * 5,
        scratch_shapes=[
            bv(UNITS, width, width), bv(2, line, 2, unit_rows, width), bv(2, line, unit_rows, width),
            bv(line, unit_rows, width), bv(4, line, part, strip), bv(4, reps, part, strip), fv(2, unit_rows, width),
            bv(line, rows, width), bv(line, rows, width), bv(frames, width), bv(line, fr, width), bv(line, fr, width),
            bv(line, fr, width), fv(shards, GRAD_ROWS, 128), fv(shards, GRAD_ROWS, 128), fv(reps, GRAD_ROWS, 128),
            fv(GRAD_ROWS, width), fv(rows, width), fv(rows, width),
            bv(3, rows, width), bv(2, rows, width), bv(2, rows, width), bv(width, rows),
            bv(pairs, 2 * rows, 128), fv(8, 2 * rows), fv(pairs, 128, 2 * rows), bv(rows, width), bv(rows, width),
            fv(width, width), fv(width, width),
            dma((3, 2)), dma((UNITS,)), dma((2,)), dma((max(reps, 2),)), dma((most,)), dma((most,)), dma((most,)),
            dma((most, reps)), dma((most, reps)), dma((most, line)), dma((most, line)), dma((most, reps)), dma((most, reps)),
            dma((line,)), dma((line,)), dma((line,)), dma((line,)), dma((line,)), dma((line,)), dma((line,)), dma((line,)),
            dma((shards,)), dma((shards,)), dma((reps,)), dma((reps,)),
        ],
        compiler_params=pltpu.CompilerParams(
            collective_id=1, has_side_effects=True, vmem_limit_bytes=62 * 2**20
        ),
        name="backward",
    )(ffn, hidden, states, keys, values, c_keys, c_values, keep_self, keep_cross, *saved)


def local(
    shards, reps, hidden, encoded, tok_seg, seg_parent, self_qkv, self_out, cross_qkv, cross_out,
    fc_in, fc_out, proj_bias, out_bias, fc_in_bias, norm_gain, norm_bias, cotangent,
):
    rows, width = hidden.shape
    strip = norm_gain.shape[1]
    small = jnp.concatenate(
        [proj_bias, out_bias, fc_in_bias.reshape(UNITS, strip), norm_gain, norm_bias], axis=0
    )
    small = jnp.pad(small, ((0, SMALL_ROWS - small.shape[0]), (0, 128 - strip)))
    ids = jnp.arange(128, dtype=jnp.int32)
    parents = jnp.pad(seg_parent[0], (0, 128 - seg_parent.shape[1]), constant_values=-1)
    parents = (parents[:, None] == ids[None, :]).astype(BF)

    (result, grad_across, ffn, keys, values, queries, hot, lse, att, c_queries, c_keys, c_values, c_lse, catt,
     after_self, normed1, sums, params, w_self, w_cross, all_hidden, states) = forward(
        (shards, reps), self_qkv, self_out, cross_qkv, cross_out, fc_in, fc_out, hidden, encoded, small, tok_seg, parents, cotangent,
    )
    d_hidden, d_encoded, vector_sum, total = backward(
        (shards, reps), ffn, all_hidden, states, keys, values, c_keys, c_values, w_self, w_cross,
        params, grad_across, queries, hot, lse, att, c_queries, c_lse, catt, after_self, normed1, sums,
    )[:4]
    vector_sum = vector_sum[:, :strip]
    by_unit = total.reshape(4, UNITS, strip, width)
    return (
        result, d_hidden, d_encoded,
        by_unit[3, :3], by_unit[3, 3], by_unit[2, :3], by_unit[2, 3],
        jnp.transpose(by_unit[1], (1, 0, 2)).reshape(strip, UNITS * width), total[0],
        vector_sum[0:4], vector_sum[4:7], vector_sum[13:17].reshape(UNITS * strip),
        vector_sum[7:10], vector_sum[10:13],
    )


def solution(mesh):
    across = P(("rep", "shard"), None)
    matrix, matrices, vectors = P("shard", None), P(None, "shard", None), P(None, "shard")
    return jax.shard_map(
        functools.partial(local, mesh.shape["shard"], mesh.shape["rep"]),
        mesh=mesh,
        in_specs=(
            across, across, P("rep", None), P("rep", None), matrices, matrix, matrices, matrix, matrix, matrix,
            vectors, vectors, P("shard"), vectors, vectors, across,
        ),
        out_specs=(
            across, across, across, matrices, matrix, matrices, matrix, matrix, matrix,
            vectors, vectors, P("shard"), vectors, vectors,
        ),
        check_vma=False,
    )
```

```python
import functools
import math

import jax
import jax.numpy as jnp
from jax import lax
from jax.experimental import pallas as pl
from jax.experimental.pallas import tpu as pltpu
from jax.sharding import PartitionSpec as P

HEADS = 12
EPS = 1e-05
NEGATIVE = -1e30
MESH = pl.DeviceIdType.MESH
UNITS = 4
SMALL_ROWS = 32
GRAD_ROWS = 24
BF = jnp.bfloat16
F32 = jnp.float32


def flip_bit(index, bit):
    size = 1 << bit
    return index + size * (1 - 2 * ((index // size) % 2))


def pick(core, first, second):
    return first + core * (second - first)


class Place:
    def __init__(self, shards, reps):
        self.shards, self.reps = shards, reps
        self.rep = lax.axis_index("rep")
        self.shard = lax.axis_index("shard")
        self.pos = self.shard // 2
        self.core = self.shard % 2
        self.line = shards // 2
        self.bits = reps.bit_length() - 1

    def partner(self):
        return (self.rep, self.shard + 1 - 2 * self.core)

    def along(self, pos):
        return (self.rep, pos * 2 + self.core)

    def flipped(self, index, step):
        return pick(
            self.core, flip_bit(index, step), flip_bit(index, self.bits - 1 - step)
        )

    def subset(self, index, steps):
        for step in steps:
            index = self.flipped(index, step)
        return index


def subsets(steps):
    found = [()]
    for step in steps:
        found = found + [more + (step,) for more in found]
    return found


def remote(src, dst, send, recv, device):
    return pltpu.make_async_remote_copy(
        src_ref=src, dst_ref=dst, send_sem=send, recv_sem=recv,
        device_id=device, device_id_type=MESH,
    )


def greet(devices, conditions):
    barrier = pltpu.get_barrier_semaphore()
    count = 0
    for device, condition in zip(devices, conditions):
        if condition is None:
            pl.semaphore_signal(barrier, inc=1, device_id=device, device_id_type=MESH)
            count = count + 1
        else:
            @pl.when(condition)
            def _(device=device):
                pl.semaphore_signal(barrier, inc=1, device_id=device, device_id_type=MESH)
            count = count + jnp.where(condition, 1, 0)
    pl.semaphore_wait(barrier, count)


def cond(condition, action):
    @pl.when(condition)
    def _():
        action()


def nn(a, b):
    return lax.dot_general(a, b, (((1,), (0,)), ((), ())), preferred_element_type=F32)


def nt(a, b):
    return lax.dot_general(a, b, (((1,), (1,)), ((), ())), preferred_element_type=F32)


def normalise(values):
    centered = values - jnp.mean(values, axis=-1, keepdims=True)
    scale = lax.rsqrt(jnp.mean(centered * centered, axis=-1, keepdims=True) + EPS)
    return centered * scale, scale


def norm_back(hat, scale, gain, grad):
    scaled = grad * gain
    mean = jnp.mean(scaled, axis=-1, keepdims=True)
    along = jnp.mean(scaled * hat, axis=-1, keepdims=True)
    return (scaled - mean - hat * along) * scale


def column_sums(values):
    return jnp.sum(values, axis=0, keepdims=True)


def pair_rows(values, pair):
    both = values[:, pair * 128 : pair * 128 + 128]
    first = lax.broadcasted_iota(jnp.int32, both.shape, 1) < 64
    zero = jnp.zeros_like(both)
    return jnp.concatenate([jnp.where(first, both, zero), jnp.where(first, zero, both)], axis=0)


def unpair(turned):
    both = jnp.transpose(turned)
    rows = both.shape[0] // 2
    first = lax.broadcasted_iota(jnp.int32, (rows, 128), 1) < 64
    return jnp.where(first, both[:rows], both[rows:])


def earlier(block, rows):
    key = lax.broadcasted_iota(jnp.int32, (block, 2 * rows), 0)
    query = lax.broadcasted_iota(jnp.int32, (block, 2 * rows), 1)
    return key <= jnp.where(query >= rows, query - rows, query)


def attend_start(top, total, acc):
    top[...] = jnp.full(top.shape, NEGATIVE, F32)
    total[...] = jnp.zeros(total.shape, F32)
    acc[...] = jnp.zeros(acc.shape, F32)


def attend_block(queries, keys, turned_values, hot, top, total, acc, diagonal):
    for pair in range(queries.shape[0]):
        lanes = slice(pair * 128, pair * 128 + 128)
        left = keys[:, lanes]
        if hot is not None:
            left = jnp.concatenate([left, hot], axis=1)
        scores = nt(left, queries[pair])
        if diagonal:
            scores = jnp.where(earlier(left.shape[0], scores.shape[1] // 2), scores, NEGATIVE)
        before = top[pair : pair + 1, :]
        after = jnp.maximum(before, jnp.max(scores, axis=0, keepdims=True))
        factor = jnp.exp(before - after)
        weights = jnp.exp(scores - after)
        top[pair : pair + 1, :] = after
        total[pair : pair + 1, :] = total[pair : pair + 1, :] * factor + jnp.sum(weights, axis=0, keepdims=True)
        acc[pair] = acc[pair] * factor + nn(turned_values[lanes, :], weights.astype(BF))


def attend_finish(top, total, acc, lse, out):
    for pair in range(acc.shape[0]):
        sums = total[pair : pair + 1, :]
        lse[pair : pair + 1, :] = top[pair : pair + 1, :] + jnp.log(sums)
        out[:, pair * 128 : pair * 128 + 128] = unpair(acc[pair] / sums)


def attend_back_block(queries, grads, keys, values, turned_keys, hot, lse, delta, grad_q, grad_k, grad_v, diagonal):
    for pair in range(queries.shape[0]):
        lanes = slice(pair * 128, pair * 128 + 128)
        left = keys[:, lanes]
        if hot is not None:
            left = jnp.concatenate([left, hot], axis=1)
        scores = nt(left, queries[pair])
        if diagonal:
            scores = jnp.where(earlier(left.shape[0], scores.shape[1] // 2), scores, NEGATIVE)
        probs = jnp.exp(scores - lse[pair : pair + 1, :])
        grad_probs = nt(values[:, lanes], grads[pair])
        grad_scores = (probs * (grad_probs - delta[pair : pair + 1, :])).astype(BF)
        grad_v[:, lanes] = nn(probs.astype(BF), grads[pair]).astype(BF)
        grad_k[:, lanes] = nn(grad_scores, queries[pair, :, 0:128]).astype(BF)
        grad_q[pair] += nn(turned_keys[lanes, :], grad_scores)


def deltas(grad, out, delta, pairs):
    turned = jnp.transpose(grad.astype(F32) * out)
    for pair in range(pairs):
        at = pair * 128
        one = jnp.sum(turned[at : at + 64], axis=0, keepdims=True)
        two = jnp.sum(turned[at + 64 : at + 128], axis=0, keepdims=True)
        delta[pair : pair + 1, :] = jnp.concatenate([one, two], axis=1)


def store_owners(grads, group, unit, matrix, shards):
    rows = matrix.shape[0] // shards
    for s in range(shards):
        grads[group, s // 2, s % 2, unit * rows : (unit + 1) * rows, :] = matrix[s * rows : (s + 1) * rows].astype(BF)


def erf_parts(pre):
    cdf = 0.5 * (1.0 + lax.erf(pre * (0.5**0.5)))
    slope = cdf + pre * jnp.exp(-0.5 * pre * pre) * (1.0 / math.sqrt(2.0 * math.pi))
    return cdf, slope


G_OUT, G_IN, G_CROSS, G_SELF = range(4)
V_PROJ, V_OUT, V_GAIN, V_SHIFT, V_IN = 0, 4, 7, 10, 13


def shape_of(kind, *shape):
    return jax.ShapeDtypeStruct(shape, kind)


SELF, CROSS, FC_IN, FC_OUT, HIDDEN, ENCODED, SMALL = range(7)
WEIGHTS = (SELF, CROSS, FC_IN, FC_OUT)


def forward_kernel(
    shards, reps, *refs,
):
    qkv_out = {0: refs[0:2], 1: refs[2:4]}
    ins = (refs[0], refs[2], *refs[4:9])
    segs, parents, cotangent = refs[9:12]
    (result, grad_across, grads, keys, values, queries, hot, lse, att, c_queries, c_keys, c_values, c_lse, catt,
     after_self, normed1, sums, params, keep_self, keep_cross, keep_hidden, keep_states) = refs[12:34]
    (w_self, w_cross, w_in, w_out, hidden, states, small_all, bias_in,
     kbuf, vbuf, turned, c_turned, top, total, acc, grad_n2, held, gbuf_in, gbuf_out,
     k_sem, v_sem, g_sem, keep_sem, own_sem, mate_send, mate_recv, line_send, line_recv, rep_send, rep_recv,
     far_send, far_recv, small_send, small_recv) = refs[34:]
    outs = (w_self, w_cross, w_in, w_out, hidden, states, small_all)
    here = Place(shards, reps)
    line, bits = here.line, here.bits
    pos, core, rep, shard = here.pos, here.core, here.rep, here.shard
    rows, width = cotangent.shape
    frames = states.shape[0]
    strip = width * UNITS // reps
    w_rows = ins[SELF].shape[1]


    def block(refs_, item, s):
        ref = refs_[item]
        if item in (SELF, CROSS):
            return ref.at[:, pl.ds(pl.multiple_of(s * w_rows, 16), w_rows), :]
        n = ins[item].shape[0]
        return ref.at[pl.ds(pl.multiple_of(s * n, 16), n), :]

    def piece(refs_, item, r, s):
        if item == ENCODED:
            return block(refs_, item, s)
        ref = refs_[item]
        unit = r % UNITS
        at = 0 if reps == UNITS else pl.multiple_of((r // UNITS) * strip, 128)
        columns = pl.ds(at, strip)
        if item in (SELF, CROSS):
            return ref.at[unit, pl.ds(pl.multiple_of(s * w_rows, 16), w_rows), columns]
        if item == FC_IN:
            return ref.at[
                pl.ds(pl.multiple_of(s * w_rows, 16), w_rows), pl.ds(pl.multiple_of(unit * width + at, 128), strip)
            ]
        return ref.at[pl.ds(pl.multiple_of(s * UNITS * w_rows + unit * w_rows, 16), w_rows), columns]

    mate = here.partner()
    greet(
        [(rep, (shard + d) % shards) for d in range(1, shards)]
        + [(flip_bit(rep, bit), shard) for bit in range(bits)],
        [None] * (shards - 1 + bits),
    )

    def own_parts(item):
        qkv, last_one = qkv_out[item]
        at = pl.ds(pl.multiple_of(shard * w_rows, 16), w_rows)
        return [
            pltpu.make_async_copy(qkv, outs[item].at[pl.ds(0, UNITS - 1), at, :], own_sem.at[item]),
            pltpu.make_async_copy(last_one, outs[item].at[UNITS - 1, at, :], own_sem.at[7 + item]),
        ]

    own = {i: pltpu.make_async_copy(ins[i], block(outs, i, shard), own_sem.at[i]) for i in range(2, 6)}
    own[SMALL] = pltpu.make_async_copy(ins[SMALL], small_all.at[shard], own_sem.at[SMALL])
    to_mate = [
        remote(
            block(outs, i, shard) if i in qkv_out else ins[i], block(outs, i, shard), mate_send.at[i], mate_recv.at[i], mate
        )
        for i in range(6)
    ]
    small_out = [
        remote(ins[SMALL], small_all.at[shard], small_send.at[d], small_recv.at[d], (rep, (shard + d) % shards))
        for d in range(1, shards)
    ]

    def small_wait(d):
        s = (shard - d + shards) % shards
        remote(small_all.at[s], small_all.at[s], small_send.at[d], small_recv.at[d], mate).wait_recv()

    WAYS = (0, 1)

    def source(way, t):
        return (pos - t if way == 0 else pos + t) * 2 + core

    def arrives(way, t):
        return pos - t >= 0 if way == 0 else pos + t < line

    def onward(way):
        return pos + 1 < line if way == 0 else pos > 0

    def line_copy(item, way, t):
        region = piece(outs, item, rep, source(way, t))
        at = (item, way * line + t)
        return remote(
            piece(ins, item, rep, 0) if t == 0 and item not in qkv_out else region, region, line_send.at[at], line_recv.at[at],
            here.along(pos + 1 if way == 0 else pos - 1),
        )

    def take(item, way, t):
        region = piece(outs, item, rep, source(way, t))
        at = (item, way * line + t - 1)
        remote(region, region, line_send.at[at], line_recv.at[at], mate).wait_recv()
        if t + 1 < line:
            cond(onward(way), lambda: line_copy(item, way, t).start())

    def each_source(action):
        for t in range(1, line):
            for way in WAYS:
                cond(arrives(way, t), functools.partial(action, way, t))

    def hop(t):
        s = (pos - t) * 2 + core
        src = ins[HIDDEN] if t == 0 else block(outs, HIDDEN, s)
        return remote(
            src, block(outs, HIDDEN, s), line_send.at[HIDDEN, t], line_recv.at[HIDDEN, t], here.along(pos + 1)
        )

    def hop_wait(t):
        region = block(outs, HIDDEN, (pos - t) * 2 + core)
        remote(region, region, line_send.at[HIDDEN, t - 1], line_recv.at[HIDDEN, t - 1], mate).wait_recv()

    def far(item, at, s):
        return remote(block(outs, item, s), block(outs, item, s), far_send.at[item, at], far_recv.at[item, at], mate)

    def mate_block(s):
        return s + 1 - 2 * core

    def relay(t):
        def arrived():
            hop_wait(t)
            if t + 1 < line:
                cond(pos + 1 < line, lambda: hop(t).start())
            far(HIDDEN, t, (pos - t) * 2 + core).start()

        cond(pos - t >= 0, arrived)

    def relay_wait(t):
        far(HIDDEN, t, (pos - t) * 2 + 1 - core).wait_recv()

    def rep_at(step, more):
        return (1 << step) - 1 + subsets(range(step)).index(more)

    def rep_copy(item, way, t, step, more):
        region = piece(outs, item, here.subset(rep, more), source(way, t))
        at = (item, way * line + t, rep_at(step, more))
        return remote(region, region, rep_send.at[at], rep_recv.at[at], (here.flipped(rep, step), shard))

    def rep_wait(item, way, t, step, more):
        region = piece(outs, item, here.subset(here.flipped(rep, step), more), source(way, t))
        at = (item, way * line + t, rep_at(step, more))
        remote(region, region, rep_send.at[at], rep_recv.at[at], mate).wait_recv()

    def spread(item, step):
        def one(way, t):
            if step == 0:
                take(item, way, t)
            else:
                for more in subsets(range(step - 1)):
                    rep_wait(item, way, t, step - 1, more)
            if step < bits:
                for more in subsets(range(step)):
                    rep_copy(item, way, t, step, more).start()
            else:
                far(item, way * line + t, source(way, t)).start()

        each_source(one)

    def pass_on(item):
        def one(way, t):
            take(item, way, t)
            far(item, way * line + t, source(way, t)).start()

        each_source(one)

    def complete(item):
        if item not in qkv_out:
            own[item].wait()
        to_mate[item].wait_recv()
        each_source(lambda way, t: far(item, way * line + t, mate_block(source(way, t))).wait_recv())


    for item in (SELF, CROSS):
        for copy in own_parts(item):
            copy.start()
    own[SMALL].start()
    for copy in small_out:
        copy.start()
    for copy in own_parts(SELF):
        copy.wait()

    def send(item):
        for way in WAYS:
            cond(onward(way), lambda: line_copy(item, way, 0).start())

    send(SELF)
    cond(pos + 1 < line, lambda: hop(0).start())
    for copy in own_parts(CROSS):
        copy.wait()
    for i in (SELF, HIDDEN, CROSS, FC_IN, FC_OUT, ENCODED):
        to_mate[i].start()
        if i not in qkv_out:
            own[i].start()
    for item in (CROSS, FC_IN, FC_OUT, ENCODED):
        send(item)


    pairs = width // 128
    scale = 64 ** (-0.5)
    own_rows = pl.ds(pl.multiple_of(shard * rows, rows), rows)

    def block_of(b):
        return pl.ds(pl.multiple_of(b * rows, rows), rows)

    def gain(i):
        return params[11 + i : 12 + i, :]

    def shift(i):
        return params[14 + i : 15 + i, :]

    def write_k(b, slot):
        return pltpu.make_async_copy(kbuf.at[slot], keys.at[block_of(b)], k_sem.at[slot])

    def write_v(b, slot):
        return pltpu.make_async_copy(vbuf.at[slot], values.at[block_of(b)], v_sem.at[slot])

    count = segs.shape[1]
    ids = lax.broadcasted_iota(jnp.int32, (128, rows), 0)
    for b in range(count // rows):
        at = slice(b * rows, (b + 1) * rows)
        hot[at, :] = jnp.transpose((ids == segs[:, at]).astype(F32)).astype(BF)
    link = parents[...]
    line_ = lax.broadcasted_iota(jnp.int32, (128, 128), 0)
    across_ = lax.broadcasted_iota(jnp.int32, (128, 128), 1)
    reach = jnp.where(line_ == across_, 1.0, 0.0) + link.astype(F32) + nn(link, link)
    seen = nn(hot[own_rows, :], reach.astype(BF))
    hide = jnp.where(seen > 0.5, 0.0, NEGATIVE).astype(BF)
    hide = jnp.concatenate([hide, hide], axis=0)
    attend_start(top, total, acc)
    sums[...] = jnp.zeros_like(sums)
    grad_n2[...] = jnp.zeros_like(grad_n2)

    own[SMALL].wait()
    for d in range(1, shards):
        small_wait(d)
    part = width // shards
    for s in range(shards):
        some = small_all[s].astype(F32)
        params[:, s * part : (s + 1) * part] = some[:, :part]
        for u in range(UNITS):
            at = s * part * UNITS + u * part
            bias_in[:, at : at + part] = some[7 + u : 8 + u, :part]

    def norm0(values_):
        hat, _ = normalise(values_.astype(F32))
        return (hat * gain(0) + shift(0)).astype(BF)

    spread(SELF, 0)
    own[HIDDEN].wait()
    held[...] = norm0(hidden[own_rows, :])
    for step in range(1, bits):
        spread(SELF, step)
    relay(1)
    spread(CROSS, 0)
    spread(SELF, bits)
    to_mate[HIDDEN].wait_recv()
    complete(SELF)

    q = ((nn(held[...], w_self[0]) + params[0:1, :]).astype(BF) * scale).astype(BF)
    for pair in range(pairs):
        queries[pair, :, 0:128] = pair_rows(q, pair)
        queries[pair, :, 128:256] = hide

    def one_block(b, j, diagonal):
        slot = j % 2
        norm = held[...] if diagonal else norm0(hidden[block_of(b), :])

        @pl.when(j >= 2)
        def _():
            write_k(b, slot).wait()
            write_v(b, slot).wait()

        kbuf[slot] = nn(norm, w_self[1]).astype(BF)
        v = (nn(norm, w_self[2]) + params[1:2, :]).astype(BF)
        vbuf[slot] = v
        turned[...] = jnp.transpose(v)
        write_k(b, slot).start()
        write_v(b, slot).start()
        attend_block(queries, kbuf.at[slot], turned, hot[block_of(b), :], top, total, acc, diagonal)

    one_block(shard, jnp.int32(0), True)

    duties = {}

    def duty(j, action, *args):
        duties.setdefault(j, []).append(functools.partial(action, *args))

    last = shards - 1
    for t in range(2, line):
        duty(2 * t - 3, relay, t)
    duty(2, spread, CROSS, 1)
    duty(2, spread, FC_IN, 0)
    for step in range(2, bits + 1):
        duty(4, spread, CROSS, step)
    duty(4, spread, FC_IN, 1)
    duty(4, spread, FC_OUT, 0)
    duty(5, pass_on, ENCODED)
    for step in range(2, bits + 1):
        duty(6, spread, FC_IN, step)
    duty(7, spread, FC_OUT, 1)

    def step_block(j, carry):
        b = shard - j
        for when_, actions in sorted(duties.items()):
            @pl.when(j == when_)
            def _(actions=actions):
                for action in actions:
                    action()

        for t in range(1, line):
            @pl.when(jnp.logical_and(b >= 0, j == 2 * t - 1 + core))
            def _(t=t):
                relay_wait(t)

        @pl.when(b >= 0)
        def _():
            one_block(b, j, False)

        return carry

    lax.fori_loop(1, shards, step_block, 0)
    attend_finish(top, total, acc, lse, att)
    after_self[...] = hidden[own_rows, :].astype(F32) + nn(att[...].astype(BF), w_self[3]) + params[4:5, :]
    hat1, _ = normalise(after_self[...])
    normed1[...] = (hat1 * gain(1) + shift(1)).astype(BF)
    keep = [
        pltpu.make_async_copy(w_self, keep_self, keep_sem.at[0]),
        pltpu.make_async_copy(w_cross, keep_cross, keep_sem.at[1]),
        pltpu.make_async_copy(states, keep_states, keep_sem.at[2]),
        pltpu.make_async_copy(hidden.at[own_rows], keep_hidden.at[own_rows], keep_sem.at[3]),
    ]
    keep[0].start()
    keep[3].start()

    def keep_block(b):
        return pltpu.make_async_copy(hidden.at[block_of(b)], keep_hidden.at[block_of(b)], keep_sem.at[4 + b])

    for b in range(shards):
        cond(b < shard, lambda: keep_block(b).start())

    complete(CROSS)
    keep[1].start()
    cq = ((nn(normed1[...], w_cross[0]) + params[2:3, :]).astype(BF) * scale).astype(BF)
    for pair in range(pairs):
        c_queries[pair] = pair_rows(cq, pair)
    attend_start(top, total, acc)
    complete(ENCODED)
    keep[2].start()

    def c_block(b, carry):
        at = block_of(b)
        c_keys[at, :] = nn(states[at, :], w_cross[1]).astype(BF)
        v = (nn(states[at, :], w_cross[2]) + params[3:4, :]).astype(BF)
        c_values[at, :] = v
        c_turned[...] = jnp.transpose(v)
        attend_block(c_queries, c_keys.at[at], c_turned, None, top, total, acc, False)

        for step in range(2, bits + 1):
            @pl.when(b == min(step - 2, frames // rows - 1))
            def _(step=step):
                spread(FC_OUT, step)

        return carry

    lax.fori_loop(0, frames // rows, c_block, 0)
    attend_finish(top, total, acc, c_lse, catt)
    after_cross = after_self[...] + nn(catt[...].astype(BF), w_cross[3]) + params[5:6, :]
    hat2, scale2 = normalise(after_cross)
    normed2 = (hat2 * gain(2) + shift(2)).astype(BF)
    held[...] = normed2
    result[...] = after_cross + params[6:7, :]
    turned2 = jnp.transpose(normed2)
    each = gbuf_out.shape[1]
    complete(FC_IN)
    complete(FC_OUT)

    def send_grads(u):
        return (
            pltpu.make_async_copy(gbuf_out.at[u % 2], grads.at[0, pl.ds(u * each, each)], g_sem.at[0, u % 2]),
            pltpu.make_async_copy(gbuf_in.at[u % 2], grads.at[1, :, :, pl.ds(u * part, part)], g_sem.at[1, u % 2]),
        )

    for u in range(UNITS):
        at = slice(u * width, (u + 1) * width)
        norm2 = held[...]
        pre = nn(norm2, w_in[:, at]) + bias_in[:, at]
        cdf, slope = erf_parts(pre)
        act = (pre * cdf).astype(BF)
        result[...] += nn(act, w_out[at, :])
        grad_pre = (slope * nt(cotangent[...], w_out[at, :])).astype(BF)
        grad_n2[...] += nt(grad_pre, w_in[:, at])
        if u >= 2:
            for copy in send_grads(u - 2):
                copy.wait()
        g = nn(turned2, grad_pre)
        for s in range(shards):
            gbuf_in[u % 2, s // 2, s % 2] = g[s * part : (s + 1) * part].astype(BF)
        g = nn(jnp.transpose(act), cotangent[...])
        tall = part * UNITS
        for j in range(width // tall):
            gbuf_out[u % 2, j // 2, j % 2] = g[j * tall : (j + 1) * tall].astype(BF)
        for copy in send_grads(u):
            copy.start()
        sums[V_IN + u : V_IN + u + 1, :] = column_sums(grad_pre.astype(F32))

    grad = cotangent[...].astype(F32)
    dn = grad_n2[...]
    grad_across[...] = grad + norm_back(hat2, scale2, gain(2), dn)
    sums[V_OUT + 2 : V_OUT + 3, :] = column_sums(grad)
    sums[V_GAIN + 2 : V_GAIN + 3, :] = column_sums(dn * hat2)
    sums[V_SHIFT + 2 : V_SHIFT + 3, :] = column_sums(dn)

    for u in (UNITS - 2, UNITS - 1):
        for copy in send_grads(u):
            copy.wait()
    write_k(shard, shard % 2).wait()
    write_v(shard, shard % 2).wait()

    @pl.when(shard >= 1)
    def _():
        write_k(shard - 1, (shard + 1) % 2).wait()
        write_v(shard - 1, (shard + 1) % 2).wait()

    for copy in keep:
        copy.wait()
    for b in range(shards):
        cond(b < shard, lambda: keep_block(b).wait())
    for i in range(6):
        to_mate[i].wait_send()
    for copy in small_out:
        copy.wait_send()
    for item in WEIGHTS + (ENCODED,):
        for way in WAYS:
            cond(onward(way), lambda: line_copy(item, way, 0).wait_send())

        def drain(way, t):
            if t + 1 < line:
                cond(onward(way), lambda: line_copy(item, way, t).wait_send())
            far(item, way * line + t, source(way, t)).wait_send()
            if item in WEIGHTS:
                for step in range(bits):
                    for more in subsets(range(step)):
                        rep_copy(item, way, t, step, more).wait_send()

        each_source(drain)
    cond(pos + 1 < line, lambda: hop(0).wait_send())
    for t in range(1, line):
        def drain_tokens():
            if t + 1 < line:
                cond(pos + 1 < line, lambda: hop(t).wait_send())
            far(HIDDEN, t, (pos - t) * 2 + core).wait_send()

        cond(pos - t >= 0, drain_tokens)


def forward(mesh_shape, self_qkv, self_out, cross_qkv, cross_out, fc_in, fc_out, hidden, encoded, small, segs, parents, cotangent):
    shards, reps = mesh_shape
    line, bits = shards // 2, reps.bit_length() - 1
    rows, width = cotangent.shape
    count, frames = rows * shards, encoded.shape[0] * shards
    pairs = width // 128
    unit_rows = fc_out.shape[0]
    part = width // shards
    each = width // unit_rows // 2
    f32, bf = functools.partial(shape_of, F32), functools.partial(shape_of, BF)
    vm, hbm = pl.BlockSpec(memory_space=pltpu.VMEM), pl.BlockSpec(memory_space=pl.ANY)
    dma = pltpu.SemaphoreType.DMA

    def bv(*shape):
        return pltpu.VMEM(shape, BF)

    def fv(*shape):
        return pltpu.VMEM(shape, F32)

    return pl.pallas_call(
        functools.partial(forward_kernel, shards, reps),
        out_shape=(
            f32(rows, width), f32(rows, width), bf(2, line, 2, unit_rows, width), bf(count, width),
            bf(count, width), bf(pairs, 2 * rows, 256), bf(count, 128), f32(8, 2 * rows), f32(rows, width),
            bf(pairs, 2 * rows, 128), bf(frames, width), bf(frames, width), f32(8, 2 * rows),
            f32(rows, width), f32(rows, width), bf(rows, width), f32(GRAD_ROWS, width), f32(SMALL_ROWS, width),
            bf(UNITS, width, width), bf(UNITS, width, width), bf(count, width), bf(frames, width),
        ),
        in_specs=[hbm] * 9 + [vm] * 3,
        out_specs=[vm, vm, hbm, hbm, hbm] + [vm] * 13 + [hbm] * 4,
        scratch_shapes=[
            bv(UNITS, width, width), bv(UNITS, width, width), bv(width, UNITS * width), bv(UNITS * width, width),
            bv(count, width), bv(frames, width), bv(shards, SMALL_ROWS, 128), fv(1, UNITS * width),
            bv(2, rows, width), bv(2, rows, width), bv(width, rows), bv(width, rows),
            fv(8, 2 * rows), fv(8, 2 * rows), fv(pairs, 128, 2 * rows), fv(rows, width), bv(rows, width),
            bv(2, line, 2, part, width), bv(2, each, 2, unit_rows, width),
            dma((2,)), dma((2,)), dma((2, 2)), dma((4 + shards,)), dma((9,)), dma((7,)), dma((7,)),
            dma((6, 2 * line)), dma((6, 2 * line)), dma((4, 2 * line, reps)), dma((4, 2 * line, reps)),
            dma((6, 2 * line)), dma((6, 2 * line)), dma((shards,)), dma((shards,)),
        ],
        compiler_params=pltpu.CompilerParams(
            collective_id=0, has_side_effects=True, vmem_limit_bytes=60 * 2**20
        ),
        name="forward",
    )(self_qkv, self_out, cross_qkv, cross_out, fc_in, fc_out, hidden, encoded, small, segs, parents, cotangent)


def backward_kernel(shards, reps, *refs):
    (ffn, hidden, states, keys, values, c_keys, c_values, keep_self, keep_cross) = refs[:9]
    (params, grad_across, queries, hot, lse, att, c_queries, c_lse, catt, after_self, normed1, sums_in) = refs[9:21]
    (d_hidden, out_denc, out_small, out, got_mate, got_rep, x_mate, x_line) = refs[21:29]
    (weights, mine, accf, stage, got_line, shared, finish, x_own, x_send, d_states, e_mate, e_own, e_line,
     s_src, s_line, s_rep, sums, dn_own, grad_after_self,
     hbuf, kbuf, vbuf, turned, pair_grads, delta, grad_q, grad_k, grad_v, gk_acc, gv_acc,
     r_sem, w_sem, load_sem, stage_sem, out_sem, mate_send, mate_recv, rep_send, rep_recv, line_send, line_recv,
     share_send, share_recv, xm_send, xm_recv, xl_send, xl_recv, em_send, em_recv, el_send, el_recv,
     s_send, s_recv, t_send, t_recv) = refs[29:]
    here = Place(shards, reps)
    line, bits = here.line, here.bits
    pos, core, rep, shard = here.pos, here.core, here.rep, here.shard
    rows, width = grad_across.shape
    frames = states.shape[0]
    fr = frames // shards
    part = width // shards
    strip = width * UNITS // reps
    scale = 64 ** (-0.5)
    pairs = width // 128
    other = 1 - core
    mate = here.partner()

    halves = 2 if reps == UNITS and width % 256 == 0 else 1
    jobs = [(G_OUT, 0, strip), (G_IN, 0, strip), (G_CROSS, 0, strip)]
    jobs += [(G_SELF, h * (strip // halves), strip // halves) for h in range(halves)]

    greet(
        [(rep, (shard + d) % shards) for d in range(1, shards)]
        + [((rep + e) % reps, shard) for e in range(1, reps)],
        [None] * (shards + reps - 2),
    )

    def held(g):
        return accf.at[g] if g < 2 else mine.at[g - 2, :, core]

    def leaving(g):
        return ffn.at[g, :, other] if g < 2 else mine.at[g - 2, :, other]

    def span(job):
        g, at, size = jobs[job]
        return pl.ds(0, width) if reps != UNITS else pl.ds(at, size)

    def swap(job):
        g = jobs[job][0]
        return remote(
            leaving(g).at[:, :, span(job)], got_mate.at[g, :, :, span(job)], mate_send.at[job], mate_recv.at[job], mate
        )

    def columns(r, job):
        g, at, size = jobs[job]
        if reps == UNITS:
            return pl.ds(at, size)
        return pl.ds(pl.multiple_of((r // UNITS) * strip + at, 128), size)

    def piece(job, r):
        return held(jobs[job][0]).at[:, pl.ds(pl.multiple_of((r % UNITS) * part, 16), part), columns(r, job)]

    def plus(a, b):
        return (a.astype(F32) + b.astype(F32)).astype(BF)

    def add_all(into, other_ref):
        def add(i, carry):
            into[i] = plus(into[i], other_ref[i])
            return carry

        lax.fori_loop(0, line, add, 0)

    load = [pltpu.make_async_copy(ffn.at[g, :, core], accf.at[g], load_sem.at[g]) for g in range(2)]

    def rep_copy(job, step, more):
        g, at, size = jobs[job]
        slot = (1 << bits) - (1 << (bits - step)) + subsets(range(step + 1, bits)).index(more)
        target = here.flipped(rep, step)
        return remote(
            piece(job, here.subset(target, more)), got_rep.at[g, slot, :, :, pl.ds(at, size)],
            rep_send.at[job, slot], rep_recv.at[job, slot], (target, shard),
        ), slot

    def send_rep(job, step):
        for more in subsets(range(step + 1, bits)):
            rep_copy(job, step, more)[0].start()

    def line_copy(job, d):
        g, at, size = jobs[job]
        to = (pos + d) % line
        return remote(
            piece(job, rep).at[to], got_line.at[g, d, :, pl.ds(at, size)], line_send.at[job, d], line_recv.at[job, d],
            here.along(to),
        )

    def share_copy(job, e):
        g, at, size = jobs[job]
        own = shared.at[g, rep, :, pl.ds(at, size)]
        return remote(own, own, share_send.at[job, e], share_recv.at[job, e], ((rep + e) % reps, shard))

    def share_wait(job, e):
        g, at, size = jobs[job]
        got = shared.at[g, (rep - e + reps) % reps, :, pl.ds(at, size)]
        remote(got, got, share_send.at[job, e], share_recv.at[job, e], ((rep + e) % reps, shard)).wait_recv()

    def stage_mate(job):
        g = jobs[job][0]
        if g < 2:
            load[g].wait()
        swap(job).wait()
        staged = stage.at[:, :, span(job)]
        copy = pltpu.make_async_copy(got_mate.at[g, :, :, span(job)], staged, stage_sem.at[0])
        copy.start()
        copy.wait()
        add_all(held(g).at[:, :, span(job)], staged)
        send_rep(job, 0)

    def stage_rep(job, step):
        g, at, size = jobs[job]
        staged = []
        for i, more in enumerate(subsets(range(step + 1, bits))):
            copy, slot = rep_copy(job, step, more)
            copy.wait()
            into = stage.at[:, pl.ds((i % UNITS) * part, part), pl.ds((i // UNITS) * size, size)]
            staged.append((more, into, pltpu.make_async_copy(
                got_rep.at[g, slot, :, :, pl.ds(at, size)], into, stage_sem.at[i]
            )))
            staged[-1][2].start()
        for more, into, copy in staged:
            copy.wait()
            add_all(piece(job, here.subset(rep, more)), into)
        if step + 1 < bits:
            send_rep(job, step + 1)
        else:
            for d in range(1, line):
                line_copy(job, d).start()

    def stage_line(job):
        g, at, size = jobs[job]
        total = piece(job, rep)[pos].astype(F32)
        for d in range(1, line):
            line_copy(job, d).wait()
            total = total + got_line[g, d, :, at : at + size].astype(F32)
        shared[g, rep, :, at : at + size] = total.astype(BF)
        for e in range(1, reps):
            share_copy(job, e).start()

    def out_copy(job):
        g = jobs[job][0]
        return pltpu.make_async_copy(finish.at[job % 2, :, span(job)], out.at[g, :, span(job)], out_sem.at[job])

    def stage_share(job):
        g, at, size = jobs[job]
        for e in range(1, reps):
            share_copy(job, e).wait_send()
            share_wait(job, e)
        if job >= 2:
            out_copy(job - 2).wait()
        for r in range(reps):
            unit, first = r % UNITS, (r // UNITS) * strip + at
            finish[job % 2, unit * part : (unit + 1) * part, first : first + size] = (
                shared[g, r, :, at : at + size].astype(F32)
            )
        out_copy(job).start()


    def x_swap(at):
        return remote(x_send.at[at], x_mate.at[at], xm_send.at[at], xm_recv.at[at], mate)

    def x_down(t):
        return remote(x_own.at[pos - t], x_line.at[t - 1], xl_send.at[t], xl_recv.at[t - 1], here.along(pos - 1))

    def x_flush(t):
        def flush():
            at = pos - t
            x_swap(at).wait()
            copy = pltpu.make_async_copy(x_mate.at[at], hbuf.at[2], stage_sem.at[0])
            copy.start()
            copy.wait()
            x_own[at] = plus(x_own[at], hbuf[2])

        cond(pos - t >= 0, flush)

    def x_chain(t):
        def link_():
            def take():
                remote(x_line.at[t], x_line.at[t], xl_send.at[t], xl_recv.at[t], mate).wait_recv()
                copy = pltpu.make_async_copy(x_line.at[t], hbuf.at[2], stage_sem.at[0])
                copy.start()
                copy.wait()
                x_own[pos - t] = plus(x_own[pos - t], hbuf[2])

            if t + 1 < line:
                cond(pos + 1 < line, take)
            if t > 0:
                x_down(t).start()

        cond(pos - t >= 0, link_)

    top_end = pos == line - 1


    def e_swap(i):
        return remote(
            d_states.at[pl.ds(pl.multiple_of((2 * i + other) * fr, 16), fr)], e_mate.at[i], em_send.at[i], em_recv.at[i],
            mate,
        )

    def e_out(d):
        to = (pos + d) % line
        return remote(e_own.at[to], e_line.at[d], el_send.at[d], el_recv.at[d], here.along(to))

    def e_stage():
        for i in range(line):
            e_swap(i).wait()
            mine_rows = d_states[pl.ds(pl.multiple_of((2 * i + core) * fr, 16), fr), :]
            e_own[i] = plus(mine_rows, e_mate[i])
        for d in range(1, line):
            e_out(d).start()

    def e_finish():
        total = e_own[pos].astype(F32)
        for d in range(1, line):
            e_out(d).wait()
            total = total + e_line[d].astype(F32)
        out_denc[...] = total


    def s_out(d):
        to = (shard + d) % shards
        return remote(s_src.at[to], s_line.at[d], s_send.at[d], s_recv.at[d], (rep, to))

    def s_share(e):
        return remote(s_rep.at[rep], s_rep.at[rep], t_send.at[e], t_recv.at[e], ((rep + e) % reps, shard))

    def s_start():
        for s in range(shards):
            s_src[s, 0:13, 0:part] = sums[0:13, s * part : (s + 1) * part]
            for u in range(UNITS):
                at = (s * UNITS + u) * part
                row = V_IN + at // width
                s_src[s, V_IN + u : V_IN + u + 1, 0:part] = sums[row : row + 1, at % width : at % width + part]
        for d in range(1, shards):
            s_out(d).start()

    def s_middle():
        total = s_src[shard]
        for d in range(1, shards):
            s_out(d).wait()
            total = total + s_line[d]
        s_rep[rep] = total
        for e in range(1, reps):
            s_share(e).start()

    def s_finish():
        for e in range(1, reps):
            s_share(e).wait_send()
            got = s_rep.at[(rep - e + reps) % reps]
            remote(got, got, t_send.at[e], t_recv.at[e], ((rep + e) % reps, shard)).wait_recv()
        total = s_rep[0]
        for r in range(1, reps):
            total = total + s_rep[r]
        out_small[...] = total


    for g in range(2):
        swap(g).start()
        load[g].start()

    def block_of(b):
        return pl.ds(pl.multiple_of(b * rows, rows), rows)

    def reads(cross, b, slot):
        sources = (states, c_keys, c_values) if cross else (hidden, keys, values)
        return [
            pltpu.make_async_copy(src.at[block_of(b)], buf.at[slot], r_sem.at[i, slot])
            for i, (src, buf) in enumerate(zip(sources, (hbuf, kbuf, vbuf)))
        ]

    def weight(source, unit):
        return pltpu.make_async_copy(source.at[unit], weights.at[unit], w_sem.at[unit])

    for unit in (3, 1, 2, 0):
        weight(keep_cross, unit).start()
    for copy in reads(True, 0, 0):
        copy.start()

    def gain(i):
        return params[11 + i : 12 + i, :]

    s_src[...] = jnp.zeros_like(s_src)
    sums[...] = sums_in[...]
    grad = grad_across[...]
    branch = grad.astype(BF)
    sums[V_OUT + 1 : V_OUT + 2, :] = column_sums(branch.astype(F32))
    store_owners(mine, 0, 3, nn(jnp.transpose(catt[...].astype(BF)), branch), shards)
    weight(keep_cross, 3).wait()
    g_catt = nt(branch, weights[3]).astype(BF)
    weight(keep_self, 3).start()
    deltas(g_catt, catt[...], delta, pairs)
    for pair in range(pairs):
        pair_grads[pair] = pair_rows(g_catt, pair)
    grad_q[...] = jnp.zeros_like(grad_q)
    gk_acc[...] = jnp.zeros_like(gk_acc)
    gv_acc[...] = jnp.zeros_like(gv_acc)
    sums[V_PROJ + 3 : V_PROJ + 4, :] = jnp.zeros((1, width), F32)
    stage_mate(0)
    weight(keep_cross, 1).wait()
    weight(keep_cross, 2).wait()
    c_blocks = frames // rows

    def c_block(b, carry):
        slot = b % 2
        for copy in reads(True, b, slot):
            copy.wait()

        @pl.when(b + 1 < c_blocks)
        def _():
            for copy in reads(True, b + 1, 1 - slot):
                copy.start()

        turned[...] = jnp.transpose(kbuf[slot])
        attend_back_block(
            c_queries, pair_grads, kbuf.at[slot], vbuf.at[slot], turned, None, c_lse, delta, grad_q, grad_k, grad_v, False
        )
        gk, gv = grad_k[...], grad_v[...]
        flipped = jnp.transpose(hbuf[slot])
        gk_acc[...] += nn(flipped, gk)
        gv_acc[...] += nn(flipped, gv)
        d_states[block_of(b), :] = (nt(gk, weights[1]) + nt(gv, weights[2])).astype(BF)
        sums[V_PROJ + 3 : V_PROJ + 4, :] += column_sums(gv.astype(F32))

        @pl.when(b == 0)
        def _():
            stage_mate(1)

        return carry

    lax.fori_loop(0, c_blocks, c_block, 0)
    for unit in (1, 2):
        weight(keep_self, unit).start()
    for copy in reads(False, shard, 0):
        copy.start()
    for i in range(line):
        e_swap(i).start()
    store_owners(mine, 0, 1, gk_acc[...], shards)
    store_owners(mine, 0, 2, gv_acc[...], shards)
    gcq = jnp.concatenate([(unpair(grad_q[pair]) * scale).astype(BF) for pair in range(pairs)], axis=1)
    sums[V_PROJ + 2 : V_PROJ + 3, :] = column_sums(gcq.astype(F32))
    store_owners(mine, 0, 0, nn(jnp.transpose(normed1[...]), gcq), shards)
    swap(2).start()
    weight(keep_cross, 0).wait()
    dn1 = nt(gcq, weights[0])
    weight(keep_self, 0).start()
    hat1, scale1 = normalise(after_self[...])
    sums[V_GAIN + 1 : V_GAIN + 2, :] = column_sums(dn1 * hat1)
    sums[V_SHIFT + 1 : V_SHIFT + 2, :] = column_sums(dn1)
    grad_after_self[...] = grad + norm_back(hat1, scale1, gain(1), dn1)
    stage_rep(0, 0)

    self_branch = grad_after_self[...].astype(BF)
    sums[V_OUT : V_OUT + 1, :] = column_sums(self_branch.astype(F32))
    store_owners(mine, 1, 3, nn(jnp.transpose(att[...].astype(BF)), self_branch), shards)
    weight(keep_self, 3).wait()
    g_att = nt(self_branch, weights[3]).astype(BF)
    deltas(g_att, att[...], delta, pairs)
    for pair in range(pairs):
        pair_grads[pair] = pair_rows(g_att, pair)
    grad_q[...] = jnp.zeros_like(grad_q)
    gk_acc[...] = jnp.zeros_like(gk_acc)
    gv_acc[...] = jnp.zeros_like(gv_acc)
    sums[V_PROJ + 1 : V_PROJ + 2, :] = jnp.zeros((1, width), F32)
    sums[V_GAIN : V_GAIN + 1, :] = jnp.zeros((1, width), F32)
    sums[V_SHIFT : V_SHIFT + 1, :] = jnp.zeros((1, width), F32)
    weight(keep_self, 1).wait()
    weight(keep_self, 2).wait()

    def one_block(b, j, diagonal):
        slot = j % 2
        for copy in reads(False, b, slot):
            copy.wait()

        @pl.when(b >= 1)
        def _():
            for copy in reads(False, b - 1, 1 - slot):
                copy.start()

        turned[...] = jnp.transpose(kbuf[slot])
        attend_back_block(
            queries, pair_grads, kbuf.at[slot], vbuf.at[slot], turned, hot[block_of(b), :], lse, delta,
            grad_q, grad_k, grad_v, diagonal,
        )
        hat, _ = normalise(hbuf[slot].astype(F32))
        norm = (hat * gain(0) + params[14:15, :]).astype(BF)
        gk, gv = grad_k[...], grad_v[...]
        flipped = jnp.transpose(norm)
        gk_acc[...] += nn(flipped, gk)
        gv_acc[...] += nn(flipped, gv)
        dn = nt(gk, weights[1]) + nt(gv, weights[2])

        @pl.when(b % 2 == core)
        def _():
            x_own[b // 2] = dn.astype(BF)

        @pl.when(b % 2 != core)
        def _():
            x_send[b // 2] = dn.astype(BF)
            x_swap(b // 2).start()

        sums[V_PROJ + 1 : V_PROJ + 2, :] += column_sums(gv.astype(F32))
        sums[V_GAIN : V_GAIN + 1, :] += column_sums(dn * hat)
        sums[V_SHIFT : V_SHIFT + 1, :] += column_sums(dn)

    one_block(shard, jnp.int32(0), True)

    @pl.when(core == 0)
    def _():
        x_send[pos] = jnp.zeros((rows, width), BF)
        x_swap(pos).start()

    stage_mate(2)
    duties = {}

    def duty(j, action, *args):
        duties.setdefault(max(1, min(j, shards - 1)), []).append(functools.partial(action, *args))

    last = shards - 1
    duty(2, stage_rep, 1, 0)
    for t in range(0, line - 1):
        duty(2 * t + 2, x_flush, t)
        if t > 0:
            duty(2 * t + 2, cond, top_end, functools.partial(x_chain, t))
    duty(3, e_stage)
    for step in range(1, bits):
        duty(1 + 2 * step, stage_rep, 0, step)
        duty(4 + 2 * step, stage_rep, 1, step)

    def step_block(j, carry):
        b = shard - j
        for when_, actions in sorted(duties.items()):
            @pl.when(j == when_)
            def _(actions=actions):
                for action in actions:
                    action()

        @pl.when(b >= 0)
        def _():
            one_block(b, j, False)

        return carry

    lax.fori_loop(1, shards, step_block, 0)
    store_owners(mine, 1, 1, gk_acc[...], shards)
    store_owners(mine, 1, 2, gv_acc[...], shards)
    gq = jnp.concatenate([(unpair(grad_q[pair]) * scale).astype(BF) for pair in range(pairs)], axis=1)
    sums[V_PROJ : V_PROJ + 1, :] = column_sums(gq.astype(F32))
    own_hidden = pltpu.make_async_copy(hidden.at[block_of(shard)], hbuf.at[0], r_sem.at[0, 0])
    own_hidden.start()
    own_hidden.wait()
    hat0, scale0 = normalise(hbuf[0].astype(F32))
    norm = (hat0 * gain(0) + params[14:15, :]).astype(BF)
    store_owners(mine, 1, 0, nn(jnp.transpose(norm), gq), shards)
    first_self = 3
    for job in range(first_self, len(jobs)):
        swap(job).start()
    weight(keep_self, 0).wait()
    dn = nt(gq, weights[0])
    dn_own[...] = dn
    sums[V_GAIN : V_GAIN + 1, :] += column_sums(dn * hat0)
    sums[V_SHIFT : V_SHIFT + 1, :] += column_sums(dn)
    s_start()
    selves = range(first_self, len(jobs))
    stage_rep(2, 0)
    for job in selves:
        stage_mate(job)
    x_flush(line - 1)
    cond(top_end, lambda: x_chain(line - 1))
    for step in range(1, bits):
        stage_rep(2, step)
    stage_line(0)
    stage_line(1)
    s_middle()
    for step in range(bits):
        for job in selves:
            stage_rep(job, step)
            if step == 0 and job == len(jobs) - 1:
                for t in range(1, line - 1):
                    cond(pos < line - 1, lambda: x_chain(t))
    stage_line(2)
    for job in selves:
        stage_line(job)
    stage_share(0)
    stage_share(1)
    s_finish()
    e_finish()
    x_chain(0)

    for t in range(1, line):
        cond(pos - t >= 0, lambda: x_down(t).wait_send())
    d_hidden[...] = dn_own[...] + x_own[pos].astype(F32)
    d_hidden[...] = grad_after_self[...] + norm_back(hat0, scale0, gain(0), d_hidden[...])
    stage_share(2)
    for job in selves:
        stage_share(job)
    for job in range(len(jobs) - 2, len(jobs)):
        out_copy(job).wait()


def backward(mesh_shape, ffn, hidden, states, keys, values, c_keys, c_values, keep_self, keep_cross, *saved):
    shards, reps = mesh_shape
    line, bits = shards // 2, reps.bit_length() - 1
    rows, width = saved[1].shape
    frames = states.shape[0]
    fr = frames // shards
    pairs = width // 128
    part = width // shards
    unit_rows = UNITS * part
    strip = width * UNITS // reps
    f32, bf = functools.partial(shape_of, F32), functools.partial(shape_of, BF)
    vm, hbm = pl.BlockSpec(memory_space=pltpu.VMEM), pl.BlockSpec(memory_space=pl.ANY)
    dma = pltpu.SemaphoreType.DMA
    most = 5

    def bv(*shape):
        return pltpu.VMEM(shape, BF)

    def fv(*shape):
        return pltpu.VMEM(shape, F32)

    return pl.pallas_call(
        functools.partial(backward_kernel, shards, reps),
        out_shape=(
            f32(rows, width), f32(fr, width), f32(GRAD_ROWS, 128), f32(4, unit_rows, width),
            bf(4, line, unit_rows, width), bf(4, reps, line, part, strip), bf(line, rows, width), bf(line, rows, width),
        ),
        in_specs=[hbm] * 9 + [vm] * 12,
        out_specs=[vm, vm, vm] + [hbm] * 5,
        scratch_shapes=[
            bv(UNITS, width, width), bv(2, line, 2, unit_rows, width), bv(2, line, unit_rows, width),
            bv(line, unit_rows, width), bv(4, line, part, strip), bv(4, reps, part, strip), fv(2, unit_rows, width),
            bv(line, rows, width), bv(line, rows, width), bv(frames, width), bv(line, fr, width), bv(line, fr, width),
            bv(line, fr, width), fv(shards, GRAD_ROWS, 128), fv(shards, GRAD_ROWS, 128), fv(reps, GRAD_ROWS, 128),
            fv(GRAD_ROWS, width), fv(rows, width), fv(rows, width),
            bv(3, rows, width), bv(2, rows, width), bv(2, rows, width), bv(width, rows),
            bv(pairs, 2 * rows, 128), fv(8, 2 * rows), fv(pairs, 128, 2 * rows), bv(rows, width), bv(rows, width),
            fv(width, width), fv(width, width),
            dma((3, 2)), dma((UNITS,)), dma((2,)), dma((max(reps, 2),)), dma((most,)), dma((most,)), dma((most,)),
            dma((most, reps)), dma((most, reps)), dma((most, line)), dma((most, line)), dma((most, reps)), dma((most, reps)),
            dma((line,)), dma((line,)), dma((line,)), dma((line,)), dma((line,)), dma((line,)), dma((line,)), dma((line,)),
            dma((shards,)), dma((shards,)), dma((reps,)), dma((reps,)),
        ],
        compiler_params=pltpu.CompilerParams(
            collective_id=1, has_side_effects=True, vmem_limit_bytes=62 * 2**20
        ),
        name="backward",
    )(ffn, hidden, states, keys, values, c_keys, c_values, keep_self, keep_cross, *saved)


def local(
    shards, reps, hidden, encoded, tok_seg, seg_parent, self_qkv, self_out, cross_qkv, cross_out,
    fc_in, fc_out, proj_bias, out_bias, fc_in_bias, norm_gain, norm_bias, cotangent,
):
    rows, width = hidden.shape
    strip = norm_gain.shape[1]
    small = jnp.concatenate(
        [proj_bias, out_bias, fc_in_bias.reshape(UNITS, strip), norm_gain, norm_bias], axis=0
    )
    small = jnp.pad(small, ((0, SMALL_ROWS - small.shape[0]), (0, 128 - strip)))
    ids = jnp.arange(128, dtype=jnp.int32)
    parents = jnp.pad(seg_parent[0], (0, 128 - seg_parent.shape[1]), constant_values=-1)
    parents = (parents[:, None] == ids[None, :]).astype(BF)

    (result, grad_across, ffn, keys, values, queries, hot, lse, att, c_queries, c_keys, c_values, c_lse, catt,
     after_self, normed1, sums, params, w_self, w_cross, all_hidden, states) = forward(
        (shards, reps), self_qkv, self_out, cross_qkv, cross_out, fc_in, fc_out, hidden, encoded, small, tok_seg, parents, cotangent,
    )
    d_hidden, d_encoded, vector_sum, total = backward(
        (shards, reps), ffn, all_hidden, states, keys, values, c_keys, c_values, w_self, w_cross,
        params, grad_across, queries, hot, lse, att, c_queries, c_lse, catt, after_self, normed1, sums,
    )[:4]
    vector_sum = vector_sum[:, :strip]
    by_unit = total.reshape(4, UNITS, strip, width)
    return (
        result, d_hidden, d_encoded,
        by_unit[3, :3], by_unit[3, 3], by_unit[2, :3], by_unit[2, 3],
        jnp.transpose(by_unit[1], (1, 0, 2)).reshape(strip, UNITS * width), total[0],
        vector_sum[0:4], vector_sum[4:7], vector_sum[13:17].reshape(UNITS * strip),
        vector_sum[7:10], vector_sum[10:13],
    )


def solution(mesh):
    across = P(("rep", "shard"), None)
    matrix, matrices, vectors = P("shard", None), P(None, "shard", None), P(None, "shard")
    return jax.shard_map(
        functools.partial(local, mesh.shape["shard"], mesh.shape["rep"]),
        mesh=mesh,
        in_specs=(
            across, across, P("rep", None), P("rep", None), matrices, matrix, matrices, matrix, matrix, matrix,
            vectors, vectors, P("shard"), vectors, vectors, across,
        ),
        out_specs=(
            across, across, across, matrices, matrix, matrices, matrix, matrix, matrix,
            vectors, vectors, P("shard"), vectors, vectors,
        ),
        check_vma=False,
    )
```
